512 devices in a mesh: tok: 8 (over y, core), voc: 64 (over z, x).
Axes of the slice: x: 4, y: 4, z: 16, core: 2. Of those that a mesh axis runs over, the one named last changes fastest.
Arguments:
- teacher_batch: bfloat16 [160, 5120], P('tok'), may hold values from -210 to 210
- student_batch: bfloat16 [160, 3584], P('tok'), may hold values from -140 to 140
- positions: int32 [128], P('tok'), may hold values from 0 to 19
- teacher_head: bfloat16 [5120, 81920], P('tok', 'voc'), may hold values from -0.078125 to 0.078125
- student_head: bfloat16 [3584, 81920], P('tok', 'voc'), may hold values from -0.09375 to 0.09375
Outputs:
- head_grad: bfloat16 [3584, 81920], P('tok', 'voc')
- token_loss: float32 [128], P('tok')
The draws below stay inside these ranges and needn't reach their ends.
All inputs are finite; a program needn't handle non-finite values.
Results may differ from the reference program's by a relative error of at most 0.005.
Values may be sent and summed in bfloat16 or wider, within the bound.
A program may use at most 64 MiB of HBM per device.

```python
import math
import jax
import jax.numpy as jnp

DT = 5120
DS = 3584
TOK_DEV = 16
POS_DEV = 20
TOKENS = 128
POSITIONS = 160
V = 81920


def row_scales(key, rows, lower, upper):
    return jnp.exp(jax.random.uniform(key, (rows, 1), minval=math.log(lower), maxval=math.log(upper)))


def draw_teacher_batch(key, part):
    key = jax.random.fold_in(key, 11)
    key_base, key_scale = jax.random.split(key, 2)
    base = jnp.clip(jax.random.normal(key_base, (POSITIONS, DT)), -6.0, 6.0)
    scale = row_scales(key_scale, POSITIONS, 0.4, 3.0)
    return (base * scale).astype(jnp.bfloat16)


def draw_student_batch(key, part):
    key = jax.random.fold_in(key, 12)
    key_base, key_scale = jax.random.split(key, 2)
    base = jnp.clip(jax.random.normal(key_base, (POSITIONS, DS)), -6.0, 6.0)
    scale = row_scales(key_scale, POSITIONS, 0.5, 2.0)
    return (base * scale).astype(jnp.bfloat16)


def with_ends(values, own_key, smallest, largest):
    longest = values.shape.index(max(values.shape))
    spots = []
    for shift in (0, 1):
        where = [jax.random.randint(jax.random.fold_in(own_key, axis), (), 0, length) for axis, length in enumerate(values.shape)]
        where[longest] = (where[longest] + shift) % values.shape[longest]
        spots.append(tuple(where))
    return values.at[spots[0]].set(smallest).at[spots[1]].set(largest)


def levels(rng, shape, pieces, low, high):
    gain = 1.0
    for axis_at, parts in pieces:
        heights = jax.random.uniform(jax.random.fold_in(jax.random.fold_in(rng, 6), axis_at), (parts,), jnp.float32, low / len(pieces), high / len(pieces))
        gain = gain * jnp.repeat(jnp.exp(heights), shape[axis_at] // parts).reshape((-1,) + (1,) * (len(shape) - 1 - axis_at))
    return gain


def noise(key, shape, deviation, limit, cuts=(), held_as=jnp.bfloat16):
    factor_of = levels(key, shape, cuts, -0.22, 0.18) if cuts else 1.0
    array = jax.random.normal(key, shape, jnp.float32) * deviation * factor_of
    return jnp.minimum(jnp.maximum(array, -limit), limit).astype(held_as)


def setup_inputs(seed: int = 0) -> dict:
    key_of = jax.random.split(jax.random.key(seed), 6)
    teacher_batch = draw_teacher_batch(jax.random.fold_in(key_of[5], 71), 0)
    student_batch = draw_student_batch(jax.random.fold_in(key_of[5], 71), 0)
    positions = with_ends(jax.random.randint(key_of[2], (TOKENS,), 0, POS_DEV), jax.random.fold_in(key_of[2], 1), 0, POS_DEV - 1).astype(jnp.int32)
    teacher_head = noise(key_of[3], (DT, V), DT ** -0.5, 0.078125, ((0, 8), (1, 64)))
    student_head = noise(key_of[4], (DS, V), DS ** -0.5, 0.09375, ((0, 8), (1, 64)))
    return dict(teacher_batch=teacher_batch, student_batch=student_batch, positions=positions, teacher_head=teacher_head, student_head=student_head)


def reference(teacher_batch, student_batch, positions, teacher_head, student_head):
    groups = jnp.arange(TOKENS, dtype=jnp.int32) // TOK_DEV
    chosen = (groups * POS_DEV + positions).astype(jnp.int32)
    teacher_states = jnp.take(teacher_batch, chosen, axis=0)
    student_states = jnp.take(student_batch, chosen, axis=0)
    teacher_logits = jnp.dot(teacher_states, teacher_head, preferred_element_type=jnp.float32)
    student_logits = jnp.dot(student_states, student_head, preferred_element_type=jnp.float32)
    teacher_lse = jax.nn.logsumexp(teacher_logits, axis=1)
    student_lse = jax.nn.logsumexp(student_logits, axis=1)
    teacher_prob = jnp.exp(teacher_logits - teacher_lse[:, None])
    student_prob = jnp.exp(student_logits - student_lse[:, None])
    entropy = teacher_lse - jnp.sum(teacher_prob * teacher_logits, axis=1)
    weight = jnp.exp(-2.0 * entropy / math.log(V))
    cross_mean = jnp.sum(teacher_prob * student_logits, axis=1)
    token_loss = weight * (student_lse - cross_mean - entropy)
    logit_grad = ((V / TOK_DEV) * weight[:, None] * (student_prob - teacher_prob)).astype(jnp.bfloat16)
    head_grad = jnp.dot(student_states.T, logit_grad, preferred_element_type=jnp.float32).astype(jnp.bfloat16)
    return head_grad, token_loss
```

```python
import functools
import math

import jax
import jax.numpy as jnp
from jax import lax
from jax.experimental import pallas as pl
from jax.experimental.pallas import tpu as pltpu
from jax.sharding import PartitionSpec as P

MESH = pl.DeviceIdType.MESH
F32 = jnp.float32
BF16 = jnp.bfloat16
NY, NC, NX, NZ = 4, 2, 4, 16
TOK = 16
ROWS = NY * NC * TOK
STEP = 256


def remote(src, dst, send, recv, target):
    return pltpu.make_async_remote_copy(
        src_ref=src, dst_ref=dst, send_sem=send, recv_sem=recv, device_id=target, device_id_type=MESH
    )


def combine(rows):
    tops = pltpu.roll(rows, 64, axis=1)
    top = jnp.max(tops, axis=0, keepdims=True)
    total = jnp.sum(rows * jnp.exp(tops - top), axis=0, keepdims=True)
    lane = lax.broadcasted_iota(jnp.int32, (1, 128), 1)
    return jnp.where(lane < 64, total, pltpu.roll(jnp.broadcast_to(top, (8, 128)), 64, axis=1)[:1])


def exchange_kernel(
    vocab, width_t, width_s, shard,
    tb_hbm, sb_hbm, pos_ref, th_hbm, sh_hbm,
    grad_ref, cols_ref, loss_ref,
    tb, sb, th, sh, picked, states, part, sib, chip, rs, xbuf, zbuf,
    load_sem, st_send, st_recv, sib_send, sib_recv, rs_send, rs_recv, x_send, x_recv, z_send, z_recv, g_send, g_recv,
):
    chunks = shard // STEP
    tok, voc = lax.axis_index("tok"), lax.axis_index("voc")
    y, c = tok // NC, tok % NC
    z, x = voc // NX, voc % NX

    def tok_peer(k, r):
        return (((y + k) % NY) * NC + (c + r) % NC, voc)

    def x_peer(d):
        return (tok, z * NX + (x + d) % NX)

    def z_peer(d):
        return (tok, ((z + d) % NZ) * NX + x)

    tok_peers = [(k, r) for k in (2, 1, 3, 0) for r in range(NC) if (k, r) != (0, 0)]

    loads = [
        pltpu.make_async_copy(src, dst, load_sem.at[i])
        for i, (src, dst) in enumerate(((tb_hbm, tb), (sb_hbm, sb), (th_hbm, th), (sh_hbm, sh)))
    ]
    for load in loads:
        load.start()

    barrier = pltpu.get_barrier_semaphore()
    peers = [tok_peer(k, r) for k, r in tok_peers]
    peers += [x_peer(d) for d in range(1, NX)] + [z_peer(d) for d in range(1, NZ)]
    for peer in peers:
        pl.semaphore_signal(barrier, inc=1, device_id=peer, device_id_type=MESH)

    sub = lax.broadcasted_iota(jnp.int32, (TOK, TOK), 0)
    lane = lax.broadcasted_iota(jnp.int32, (TOK, TOK), 1)
    spread = jnp.where(sub == lane, jnp.broadcast_to(pos_ref[...], (TOK, TOK)), 0).astype(F32)
    column = jnp.sum(spread, axis=1, keepdims=True).astype(jnp.int32)
    n_pos = tb.shape[0]
    onehot = (lax.broadcasted_iota(jnp.int32, (TOK, n_pos), 1) == column).astype(BF16)
    loads[0].wait()
    loads[1].wait()
    pl.semaphore_wait(barrier, len(peers))

    state_copies = {}
    for k in (2, 1, 3, 0):
        yk = (y + k) % NY
        t_off = pl.multiple_of(yk * (NC * width_t), 128)
        s_off = pl.multiple_of(yk * (NC * width_s), 128)
        t_rows = jnp.dot(onehot, tb[:, pl.ds(t_off, NC * width_t)], preferred_element_type=F32)
        s_rows = jnp.dot(onehot, sb[:, pl.ds(s_off, NC * width_s)], preferred_element_type=F32)
        for h in range(NC):
            picked[k, h, :, :width_t] = t_rows[:, h * width_t : (h + 1) * width_t].astype(BF16)
            picked[k, h, :, width_t : width_t + width_s] = s_rows[:, h * width_s : (h + 1) * width_s].astype(BF16)
        for r in range(NC):
            if (k, r) == (0, 0):
                continue
            slot = r * NY + (NY - k) % NY
            copy = remote(
                picked.at[k, (c + r) % NC],
                states.at[slot * TOK : (slot + 1) * TOK],
                st_send.at[r * NY + k],
                st_recv.at[slot],
                tok_peer(k, r),
            )
            copy.start()
            state_copies[r * NY + k] = copy
    states[:TOK] = picked[0, c]
    for copy in state_copies.values():
        copy.wait_recv()
    loads[2].wait()
    loads[3].wait()

    sib_copies, rs_copies = [], []

    def pass_on(j):
        sib_copies[j].wait_recv()
        chip[j] = part[j, : ROWS // 2] + sib[j]
        for k in (2, 1, 3):
            copy = remote(
                chip.at[j, k * TOK : (k + 1) * TOK],
                rs.at[j, k - 1],
                rs_send.at[j, k - 1],
                rs_recv.at[j, k - 1],
                tok_peer(k, 0),
            )
            copy.start()
            rs_copies.append(copy)

    for j in range(chunks):
        cols = slice(j * STEP, (j + 1) * STEP)
        part[j, :, :STEP] = jnp.dot(states[:, :width_t], th[:, cols], preferred_element_type=F32)
        part[j, :, STEP:] = jnp.dot(
            states[:, width_t : width_t + width_s], sh[:, cols], preferred_element_type=F32
        )
        copy = remote(part.at[j, ROWS // 2 :], sib.at[j], sib_send.at[j], sib_recv.at[j], tok_peer(0, 1))
        copy.start()
        sib_copies.append(copy)
        if j >= 1:
            pass_on(j - 1)
    pass_on(chunks - 1)

    cols_ref[...] = jnp.transpose(states[:, width_t : width_t + width_s].astype(F32)).astype(BF16)

    for copy in rs_copies:
        copy.wait_recv()
    t_parts, s_parts = [], []
    for j in range(chunks):
        total = (chip[j, :TOK] + rs[j, 0]) + (rs[j, 1] + rs[j, 2])
        t_parts.append(total[:, :STEP])
        s_parts.append(total[:, STEP:])
    t_log = jnp.concatenate(t_parts, axis=1)
    s_log = jnp.concatenate(s_parts, axis=1)

    top_t = jnp.max(t_log, axis=1, keepdims=True)
    top_s = jnp.max(s_log, axis=1, keepdims=True)
    shifted = jnp.exp(t_log - top_t)
    columns = [
        jnp.sum(shifted, axis=1, keepdims=True),
        jnp.sum(shifted * t_log, axis=1, keepdims=True),
        jnp.sum(shifted * s_log, axis=1, keepdims=True),
        jnp.sum(jnp.exp(s_log - top_s), axis=1, keepdims=True),
        top_t, top_t, top_t, top_s,
    ]
    sub = lax.broadcasted_iota(jnp.int32, (TOK, 128), 0)
    lane = lax.broadcasted_iota(jnp.int32, (TOK, 128), 1)
    packed = jnp.zeros((TOK, 128), F32)
    for k, value in enumerate(columns):
        packed = jnp.where(lane == sub + k * TOK, value, packed)
    row = jnp.sum(packed, axis=0, keepdims=True)

    def all_rows(buf, n, row, peer, send, recv):
        buf[n - 1 : n] = row
        copies = [
            remote(buf.at[n - 1 : n], buf.at[d - 1 : d], send.at[d - 1], recv.at[d - 1], peer(d)) for d in range(1, n)
        ]
        for copy in copies:
            copy.start()
        for copy in copies:
            copy.wait_recv()
        return copies, combine(buf[...])

    x_copies, row = all_rows(xbuf, NX, row, x_peer, x_send, x_recv)
    z_copies, row = all_rows(zbuf, NZ, row, z_peer, z_send, z_recv)

    spread = jnp.broadcast_to(row, (TOK, 128))
    sum_t, moment, cross, sum_s, top_t, top_s = (
        jnp.sum(jnp.where(lane == sub + k * TOK, spread, 0.0), axis=1, keepdims=True) for k in (0, 1, 2, 3, 4, 7)
    )
    t_lse = top_t + jnp.log(sum_t)
    s_lse = top_s + jnp.log(sum_s)
    entropy = t_lse - moment / sum_t
    weight = jnp.exp(-2.0 * entropy / math.log(vocab))
    loss = weight * (s_lse - cross / sum_t - entropy)
    grad = (vocab / TOK * weight) * (jnp.exp(s_log - s_lse) - jnp.exp(t_log - t_lse))
    grad_ref[:TOK] = grad.astype(BF16)
    g_copies = []
    for k, r in tok_peers:
        slot = r * NY + (NY - k) % NY
        copy = remote(
            grad_ref.at[:TOK],
            grad_ref.at[slot * TOK : (slot + 1) * TOK],
            g_send.at[r * NY + k],
            g_recv.at[slot],
            tok_peer(k, r),
        )
        copy.start()
        g_copies.append(copy)
    loss_ref[...] = jnp.sum(jnp.where(lane == sub, loss, 0.0), axis=0, keepdims=True)

    for copy in [*state_copies.values(), *sib_copies, *rs_copies, *x_copies, *z_copies]:
        copy.wait_send()
    for copy in g_copies:
        copy.wait()


def final_kernel(cols_ref, grad_ref, loss_in, head_ref, loss_ref):
    head_ref[...] = jnp.dot(cols_ref[...], grad_ref[...], preferred_element_type=F32).astype(BF16)
    loss_ref[...] = loss_in[:, :TOK]


def on_device(teacher_batch, student_batch, positions, teacher_head, student_head):
    width_t, shard = teacher_head.shape
    width_s = student_head.shape[0]
    vocab = shard * NX * NZ
    chunks = shard // STEP
    wide = 128 * pl.cdiv(width_t + width_s, 128)
    any_spec = pl.BlockSpec(memory_space=pl.ANY)
    vmem = pl.BlockSpec(memory_space=pltpu.VMEM)
    dma = pltpu.SemaphoreType.DMA
    grad, cols, loss = pl.pallas_call(
        functools.partial(exchange_kernel, vocab, width_t, width_s, shard),
        out_shape=(
            jax.ShapeDtypeStruct((ROWS, shard), BF16),
            jax.ShapeDtypeStruct((width_s, ROWS), BF16),
            jax.ShapeDtypeStruct((1, 128), F32),
        ),
        in_specs=[any_spec, any_spec, vmem, any_spec, any_spec],
        out_specs=(vmem, vmem, vmem),
        scratch_shapes=[
            pltpu.VMEM(teacher_batch.shape, BF16),
            pltpu.VMEM(student_batch.shape, BF16),
            pltpu.VMEM(teacher_head.shape, BF16),
            pltpu.VMEM(student_head.shape, BF16),
            pltpu.VMEM((NY, NC, TOK, wide), BF16),
            pltpu.VMEM((ROWS, wide), BF16),
            pltpu.VMEM((chunks, ROWS, 2 * STEP), F32),
            pltpu.VMEM((chunks, ROWS // 2, 2 * STEP), F32),
            pltpu.VMEM((chunks, ROWS // 2, 2 * STEP), F32),
            pltpu.VMEM((chunks, NY - 1, TOK, 2 * STEP), F32),
            pltpu.VMEM((NX, 128), F32),
            pltpu.VMEM((NZ, 128), F32),
            dma((4,)),
            dma((8,)), dma((8,)),
            dma((chunks,)), dma((chunks,)),
            dma((chunks, 3)), dma((chunks, 3)),
            dma((NX - 1,)), dma((NX - 1,)),
            dma((NZ - 1,)), dma((NZ - 1,)),
            dma((8,)), dma((8,)),
        ],
        compiler_params=pltpu.CompilerParams(
            collective_id=0, has_side_effects=True
        ),
    )(teacher_batch, student_batch, positions.reshape(1, TOK), teacher_head, student_head)
    head_grad, loss = pl.pallas_call(
        final_kernel,
        out_shape=(
            jax.ShapeDtypeStruct((width_s, shard), BF16),
            jax.ShapeDtypeStruct((1, TOK), F32),
        ),
        in_specs=[vmem] * 3,
        out_specs=(vmem, vmem),
    )(cols, grad, loss)
    return head_grad, loss.reshape(TOK)


def solution(mesh):
    in_specs = (P("tok", None), P("tok", None), P("tok"), P("tok", "voc"), P("tok", "voc"))
    out_specs = (P("tok", "voc"), P("tok"))
    return jax.shard_map(
        on_device, mesh=mesh, in_specs=in_specs, out_specs=out_specs, check_vma=False
    )
```

```python
import functools
import math

import jax
import jax.numpy as jnp
from jax import lax
from jax.experimental import pallas as pl
from jax.experimental.pallas import tpu as pltpu
from jax.sharding import PartitionSpec as P

MESH = pl.DeviceIdType.MESH
F32 = jnp.float32
BF16 = jnp.bfloat16
NY, NC, NX, NZ = 4, 2, 4, 16
TOK = 16
PAIR = NC * TOK
ROWS = NY * PAIR
PLACE = {0: 0, 1: 1, 3: 2, 2: 3}
BACK = {0: 0, 1: 3, 2: 2, 3: 1}


def slot_of(k, r):
    return PLACE[k] * NC + r


def remote(src, dst, send, recv, target):
    return pltpu.make_async_remote_copy(
        src_ref=src, dst_ref=dst, send_sem=send, recv_sem=recv, device_id=target, device_id_type=MESH
    )


def lanes(values, start):
    return pltpu.roll(values, (128 - start) % 128, axis=values.ndim - 1) if start else values


def combine(rows):
    tops = pltpu.roll(rows, 64, axis=2)
    top = jnp.max(tops, axis=0)
    total = jnp.sum(rows * jnp.exp(tops - top[None]), axis=0)
    lane = lax.broadcasted_iota(jnp.int32, total.shape, 1)
    return jnp.where(lane < 64, total, pltpu.roll(top, 64, axis=1))


def exchange_kernel(
    vocab, width_t, width_s, shard,
    tb_hbm, sb_hbm, pos_ref, th_hbm, sh_hbm,
    grad_ref, cols_ref, loss_ref,
    tb, sb, th, sh, picked, states, part, sib, chip, opp, merged, ring, logits, shifted, tops, zbuf, pbuf,
    load_sem, st_send, st_recv, sib_send, sib_recv, opp_send, opp_recv, ring_send, ring_recv,
    lg_send, lg_recv, z_sem, p_sem, go, far,
):
    tok, voc = lax.axis_index("tok"), lax.axis_index("voc")
    y, c = tok // NC, tok % NC
    z, x = voc // NX, voc % NX

    def device(k, r, dx=0, dz=0):
        return (((y + k) % NY) * NC + (c + r) % NC, ((z + dz) % NZ) * NX + (x + dx) % NX)

    def core(k, which, dx=0, dz=0):
        return (((y + k) % NY) * NC + which, ((z + dz) % NZ) * NX + (x + dx) % NX)

    loads = [
        pltpu.make_async_copy(src, dst, load_sem.at[i])
        for i, (src, dst) in enumerate(((tb_hbm, tb), (sb_hbm, sb), (th_hbm, th), (sh_hbm, sh)))
    ]
    loads[0].start()
    loads[1].start()

    barrier = pltpu.get_barrier_semaphore()
    for k in (2, 1, 3):
        pl.semaphore_signal(barrier, inc=1, device_id=core(k, 0), device_id_type=MESH)

    @pl.when(c == 1)
    def _():
        pl.semaphore_signal(barrier, inc=1, device_id=core(0, 0), device_id_type=MESH)

    loads[2].start()
    loads[3].start()

    sub = lax.broadcasted_iota(jnp.int32, (TOK, TOK), 0)
    lane = lax.broadcasted_iota(jnp.int32, (TOK, TOK), 1)
    spread = jnp.where(sub == lane, jnp.broadcast_to(pos_ref[...], (TOK, TOK)), 0).astype(F32)
    column = jnp.sum(spread, axis=1, keepdims=True).astype(jnp.int32)
    onehot = (lax.broadcasted_iota(jnp.int32, (TOK, tb.shape[0]), 1) == column).astype(BF16)
    loads[0].wait()
    loads[1].wait()

    def pick(k):
        yk = (y + k) % NY
        t_off = pl.multiple_of(yk * (NC * width_t), 128)
        s_off = pl.multiple_of(yk * (NC * width_s), 128)
        t_rows = jnp.dot(onehot, tb[:, pl.ds(t_off, NC * width_t)], preferred_element_type=F32)
        s_rows = jnp.dot(onehot, sb[:, pl.ds(s_off, NC * width_s)], preferred_element_type=F32)
        for h in range(NC):
            picked[k, h, :, :width_t] = t_rows[:, h * width_t : (h + 1) * width_t].astype(BF16)
            picked[k, h, :, width_t : width_t + width_s] = s_rows[:, h * width_s : (h + 1) * width_s].astype(BF16)

    pick(2)

    @pl.when(c == 0)
    def _():
        pl.semaphore_wait(barrier, NY * NC - 1)
        pl.semaphore_signal(go, inc=1, device_id=core(0, 1), device_id_type=MESH)

    @pl.when(c == 1)
    def _():
        pl.semaphore_wait(go, 1)

    sent = []
    arrived = {}

    def start(copy):
        copy.start()
        sent.append(copy)
        return copy

    for k in (2, 1, 3, 0):
        if k != 2:
            pick(k)
        for r in range(NC):
            if (k, r) != (0, 0):
                slot = slot_of(BACK[k], r)
                arrived[BACK[k], r] = start(remote(
                    picked.at[k, (c + r) % NC],
                    states.at[slot * TOK : (slot + 1) * TOK],
                    st_send.at[slot], st_recv.at[slot], device(k, r),
                ))
    states[:TOK] = picked[0, c]

    for dz in range(1, NZ):
        pl.semaphore_signal(barrier, inc=1, device_id=core(0, 1, 0, dz), device_id_type=MESH)
    for dx in range(1, NX):
        for k in range(NY):
            pl.semaphore_signal(barrier, inc=1, device_id=core(k, 1, dx, 0), device_id_type=MESH)

    def multiply(ks):
        first = min(PLACE[k] for k in ks) * PAIR
        rows = slice(first, first + len(ks) * PAIR)
        for m in range(2):
            if m == 0:
                part[m, rows] = jnp.dot(states[rows, :width_t], th[...], preferred_element_type=F32)
            else:
                part[m, rows] = jnp.dot(
                    states[rows, width_t : width_t + width_s], sh[...], preferred_element_type=F32
                )
            for k in ks:
                at = PLACE[k]
                sib_copies[m, k] = start(remote(
                    part.at[m, at * PAIR + TOK : (at + 1) * PAIR],
                    sib.at[m, at], sib_send.at[m, at], sib_recv.at[m, at], device(0, 1),
                ))

    def add_cores(m, k):
        sib_copies[m, k].wait_recv()
        at = PLACE[k]
        chip[m, at] = part[m, at * PAIR : at * PAIR + TOK] + sib[m, at]

    sib_copies = {}
    loads[2].wait()
    loads[3].wait()
    arrived[0, 1].wait_recv()
    multiply((0,))
    for r in range(NC):
        arrived[2, r].wait_recv()
    multiply((2,))
    for k in (1, 3):
        for r in range(NC):
            arrived[k, r].wait_recv()
    multiply((1, 3))

    opp_copies = []
    for m, k in ((0, 1), (1, 3)):
        add_cores(m, 2)
        opp_copies.append(start(remote(
            chip.at[m, PLACE[2]], opp.at[m], opp_send.at[m], opp_recv.at[m], device(k, 0)
        )))
    ring_copies = {}
    for m, k in ((1, 1), (0, 3)):
        add_cores(m, k)
        ring_copies[m, k] = start(remote(
            chip.at[m, PLACE[k]], ring.at[m, k // 2], ring_send.at[m, k // 2], ring_recv.at[m, k // 2], device(k, 0)
        ))
    for m, k in ((0, 1), (1, 3)):
        add_cores(m, k)
    for m, k in ((0, 1), (1, 3)):
        opp_copies[m].wait_recv()
        merged[m] = chip[m, PLACE[k]] + opp[m]
        ring_copies[m, k] = start(remote(
            merged.at[m], ring.at[m, k // 2], ring_send.at[m, k // 2], ring_recv.at[m, k // 2], device(k, 0)
        ))
    add_cores(0, 0)
    add_cores(1, 0)
    cols_ref[...] = jnp.transpose(states[:, width_t : width_t + width_s].astype(F32)).astype(BF16)

    for copy in ring_copies.values():
        copy.wait_recv()
    t_log = chip[0, 0] + (ring[0, 0] + ring[0, 1])
    s_log = chip[1, 0] + (ring[1, 0] + ring[1, 1])
    logits[0, 0] = t_log
    logits[0, 1] = s_log

    top_t = jnp.max(t_log, axis=1, keepdims=True)
    top_s = jnp.max(s_log, axis=1, keepdims=True)
    exp_t = jnp.exp(t_log - top_t)
    exp_s = jnp.exp(s_log - top_s)
    columns = [
        jnp.sum(exp_t, axis=1, keepdims=True),
        jnp.sum(exp_t * t_log, axis=1, keepdims=True),
        jnp.sum(exp_t * s_log, axis=1, keepdims=True),
        jnp.sum(exp_s, axis=1, keepdims=True),
        top_t, top_t, top_t, top_s,
    ]
    sub = lax.broadcasted_iota(jnp.int32, (TOK, 128), 0)
    lane = lax.broadcasted_iota(jnp.int32, (TOK, 128), 1)
    packed = jnp.zeros((TOK, 128), F32)
    for k, value in enumerate(columns):
        packed = jnp.where(lane == sub + k * TOK, value, packed)
    zbuf[0:1] = jnp.sum(packed, axis=0, keepdims=True)

    @pl.when(c == 1)
    def _():
        pl.semaphore_wait(barrier, NC * ((NZ - 1) + (NX - 1) * NY))
        pl.semaphore_signal(far, inc=1, device_id=core(0, 0), device_id_type=MESH)

    @pl.when(c == 0)
    def _():
        pl.semaphore_wait(far, 1)

    for dz in sorted(range(1, NZ), key=lambda d: -min(d, NZ - d)):
        remote(zbuf.at[0:1], zbuf.at[NZ - dz : NZ - dz + 1], z_sem.at[0], z_sem.at[1], device(0, 0, 0, dz)).start()

    lg_copies = {}

    def to_other_core(k):
        mine = slot_of(k, 0)
        lg_copies[k, 1] = start(remote(
            logits.at[mine], logits.at[slot_of(k, 1)], lg_send.at[slot_of(k, 1)], lg_recv.at[slot_of(k, 1)], device(0, 1)
        ))

    for k in (1, 3, 2):
        slot = slot_of(BACK[k], 0)
        lg_copies[BACK[k], 0] = start(remote(
            logits.at[0], logits.at[slot], lg_send.at[slot], lg_recv.at[slot], device(k, 0)
        ))
    to_other_core(0)

    def exponents(slot, values):
        for m in range(2):
            top = jnp.max(values[m], axis=1, keepdims=True)
            shifted[slot, m] = jnp.exp(values[m] - top)
            tops[slot, m] = jnp.broadcast_to(top, (TOK, 128))

    def arrive(k, r):
        lg_copies[k, r].wait_recv()
        if r == 0:
            to_other_core(k)
        slot = slot_of(k, r)
        exponents(slot, (logits[slot, 0], logits[slot, 1]))

    shifted[0, 0] = exp_t
    shifted[0, 1] = exp_s
    tops[0, 0] = jnp.broadcast_to(top_t, (TOK, 128))
    tops[0, 1] = jnp.broadcast_to(top_s, (TOK, 128))
    arrive(0, 1)
    arrive(1, 0)
    arrive(3, 0)

    pltpu.make_async_copy(zbuf.at[1:NZ], zbuf.at[1:NZ], z_sem.at[1]).wait()
    pbuf[0:1] = combine(zbuf[...].reshape(NZ, 1, 128))
    plane = [(dx, k, r) for dx in (2, 1, 3, 0) for k in (2, 1, 3, 0) for r in range(NC) if (dx, k, r) != (0, 0, 0)]
    for dx, k, r in plane:
        row = BACK[dx] * NY * NC + slot_of(BACK[k], r)
        remote(pbuf.at[0:1], pbuf.at[row : row + 1], p_sem.at[0], p_sem.at[1], device(k, r, dx)).start()

    arrive(1, 1)
    arrive(3, 1)
    arrive(2, 0)
    arrive(2, 1)

    everyone = pbuf.at[1 : NX * NY * NC]
    pltpu.make_async_copy(everyone, everyone, p_sem.at[1]).wait()
    rows = combine(pbuf[...].reshape(NX, NY * NC, 128))

    sum_t = rows
    t_lse = lanes(rows, 4 * TOK) + jnp.log(sum_t)
    s_lse = lanes(rows, 7 * TOK) + jnp.log(lanes(rows, 3 * TOK))
    entropy = t_lse - lanes(rows, TOK) / sum_t
    weight = jnp.exp(-2.0 * entropy / math.log(vocab))
    loss_ref[...] = (weight * (s_lse - lanes(rows, 2 * TOK) / sum_t - entropy))[0:1]

    lane = lax.broadcasted_iota(jnp.int32, (NY * NC, TOK, 128), 2)
    sub = lax.broadcasted_iota(jnp.int32, (NY * NC, TOK, 128), 1)

    def column_of(values):
        spread = jnp.broadcast_to(values[:, None, :], (NY * NC, TOK, 128))
        return jnp.sum(jnp.where(lane == sub, spread, 0.0), axis=2, keepdims=True)

    scale = column_of(vocab / TOK * weight)
    scale_t = scale * jnp.exp(tops[:, 0] - column_of(t_lse))
    scale_s = scale * jnp.exp(tops[:, 1] - column_of(s_lse))
    for slot in range(NY * NC):
        grad = scale_s[slot, :, 0:1] * shifted[slot, 1] - scale_t[slot, :, 0:1] * shifted[slot, 0]
        grad_ref[slot * TOK : (slot + 1) * TOK] = grad.astype(BF16)

    for copy in sent:
        copy.wait_send()
    pltpu.make_async_copy(zbuf.at[1:NZ], zbuf.at[1:NZ], z_sem.at[0]).wait()
    pltpu.make_async_copy(everyone, everyone, p_sem.at[0]).wait()


def final_kernel(pieces, cols_ref, grad_ref, loss_in, head_hbm, loss_ref, head, sem):
    rows = head.shape[0] // pieces
    copies = []
    for i in range(pieces):
        at = slice(i * rows, (i + 1) * rows)
        head[at] = jnp.dot(cols_ref[at], grad_ref[...], preferred_element_type=F32).astype(BF16)
        copy = pltpu.make_async_copy(head.at[at], head_hbm.at[at], sem.at[i])
        copy.start()
        copies.append(copy)
    loss_ref[...] = loss_in[:, :TOK]
    for copy in copies:
        copy.wait()


def on_device(teacher_batch, student_batch, positions, teacher_head, student_head):
    width_t, shard = teacher_head.shape
    width_s = student_head.shape[0]
    vocab = shard * NX * NZ
    wide = 128 * pl.cdiv(width_t + width_s, 128)
    groups = NY * NC
    any_spec = pl.BlockSpec(memory_space=pl.ANY)
    vmem = pl.BlockSpec(memory_space=pltpu.VMEM)
    dma = pltpu.SemaphoreType.DMA
    grad, cols, loss = pl.pallas_call(
        functools.partial(exchange_kernel, vocab, width_t, width_s, shard),
        out_shape=(
            jax.ShapeDtypeStruct((ROWS, shard), BF16),
            jax.ShapeDtypeStruct((width_s, ROWS), BF16),
            jax.ShapeDtypeStruct((1, 128), F32),
        ),
        in_specs=[any_spec, any_spec, vmem, any_spec, any_spec],
        out_specs=(vmem, vmem, vmem),
        scratch_shapes=[
            pltpu.VMEM(teacher_batch.shape, BF16),
            pltpu.VMEM(student_batch.shape, BF16),
            pltpu.VMEM(teacher_head.shape, BF16),
            pltpu.VMEM(student_head.shape, BF16),
            pltpu.VMEM((NY, NC, TOK, wide), BF16),
            pltpu.VMEM((ROWS, wide), BF16),
            pltpu.VMEM((2, ROWS, shard), F32),
            pltpu.VMEM((2, NY, TOK, shard), F32),
            pltpu.VMEM((2, NY, TOK, shard), F32),
            pltpu.VMEM((2, TOK, shard), F32),
            pltpu.VMEM((2, TOK, shard), F32),
            pltpu.VMEM((2, 2, TOK, shard), F32),
            pltpu.VMEM((groups, 2, TOK, shard), F32),
            pltpu.VMEM((groups, 2, TOK, shard), F32),
            pltpu.VMEM((groups, 2, TOK, 128), F32),
            pltpu.VMEM((NZ, 128), F32),
            pltpu.VMEM((NX * groups, 128), F32),
            dma((4,)),
            dma((groups,)), dma((groups,)),
            dma((2, NY)), dma((2, NY)),
            dma((2,)), dma((2,)),
            dma((2, 2)), dma((2, 2)),
            dma((groups,)), dma((groups,)),
            dma((2,)), dma((2,)),
            pltpu.SemaphoreType.REGULAR,
            pltpu.SemaphoreType.REGULAR,
        ],
        compiler_params=pltpu.CompilerParams(collective_id=0, has_side_effects=True),
    )(teacher_batch, student_batch, positions.reshape(1, TOK), teacher_head, student_head)
    pieces = 4
    head_grad, loss = pl.pallas_call(
        functools.partial(final_kernel, pieces),
        out_shape=(
            jax.ShapeDtypeStruct((width_s, shard), BF16),
            jax.ShapeDtypeStruct((1, TOK), F32),
        ),
        in_specs=[vmem] * 3,
        out_specs=(any_spec, vmem),
        scratch_shapes=[pltpu.VMEM((width_s, shard), BF16), dma((pieces,))],
    )(cols, grad, loss)
    return head_grad, loss.reshape(TOK)


def solution(mesh):
    in_specs = (P("tok", None), P("tok", None), P("tok"), P("tok", "voc"), P("tok", "voc"))
    out_specs = (P("tok", "voc"), P("tok"))
    return jax.shard_map(
        on_device, mesh=mesh, in_specs=in_specs, out_specs=out_specs, check_vma=False
    )
```

```python
import functools
import math

import jax
import jax.numpy as jnp
from jax import lax
from jax.experimental import pallas as pl
from jax.experimental.pallas import tpu as pltpu
from jax.sharding import PartitionSpec as P

MESH = pl.DeviceIdType.MESH
F32 = jnp.float32
BF16 = jnp.bfloat16
NY, NC, NX, NZ = 4, 2, 4, 16
TOK = 16
CLERK = 4
PAIR = NC * TOK
ROWS = NY * PAIR
PLACE = {0: 0, 1: 1, 3: 2, 2: 3}
BACK = {0: 0, 1: 3, 2: 2, 3: 1}


def slot_of(k, r):
    return PLACE[k] * NC + r


def remote(src, dst, send, recv, target):
    return pltpu.make_async_remote_copy(
        src_ref=src, dst_ref=dst, send_sem=send, recv_sem=recv, device_id=target, device_id_type=MESH
    )


def lanes(values, start):
    return pltpu.roll(values, (128 - start) % 128, axis=values.ndim - 1) if start else values


def combine(rows):
    tops = pltpu.roll(rows, 64, axis=2)
    top = jnp.max(tops, axis=0)
    total = jnp.sum(rows * jnp.exp(tops - top[None]), axis=0)
    lane = lax.broadcasted_iota(jnp.int32, total.shape, 1)
    return jnp.where(lane < 64, total, pltpu.roll(top, 64, axis=1))


def exchange_kernel(
    vocab, width_t, width_s, shard,
    tb_hbm, sb_hbm, pos_hbm, th_hbm, sh_hbm,
    grad_ref, cols_ref, loss_ref,
    tb, sb, pos, th, sh, picked, states, part, sib, chip, opp, merged, ring, logits, shifted, tops, zbuf, pbuf,
    load_sem, st_send, st_recv, sib_send, sib_recv, opp_send, opp_recv, ring_send, ring_recv,
    lg_send, lg_recv, z_sem, p_sem, go, far,
):
    tok, voc = lax.axis_index("tok"), lax.axis_index("voc")
    y, c = tok // NC, tok % NC
    z, x = voc // NX, voc % NX

    def device(k, r, dx=0, dz=0):
        return (((y + k) % NY) * NC + (c + r) % NC, ((z + dz) % NZ) * NX + (x + dx) % NX)

    loads = [
        pltpu.make_async_copy(src, dst, load_sem.at[i])
        for i, (src, dst) in enumerate(((pos_hbm, pos), (tb_hbm, tb), (sb_hbm, sb), (th_hbm, th), (sh_hbm, sh)))
    ]
    for load in loads[:3]:
        load.start()

    barrier = pltpu.get_barrier_semaphore()
    clerk = tok == CLERK
    for k, r in ((2, 0), (2, 1), (1, 0), (1, 1), (3, 0), (3, 1), (0, 1)):
        @pl.when(device(k, r)[0] != CLERK)
        def _():
            pl.semaphore_signal(barrier, inc=1, device_id=device(k, r), device_id_type=MESH)

    for load in loads[3:]:
        load.start()

    loads[0].wait()
    sub = lax.broadcasted_iota(jnp.int32, (TOK, TOK), 0)
    lane = lax.broadcasted_iota(jnp.int32, (TOK, TOK), 1)
    spread = jnp.where(sub == lane, jnp.broadcast_to(pos[...], (TOK, TOK)), 0).astype(F32)
    column = jnp.sum(spread, axis=1, keepdims=True).astype(jnp.int32)
    onehot = (lax.broadcasted_iota(jnp.int32, (TOK, tb.shape[0]), 1) == column).astype(BF16)
    loads[1].wait()
    loads[2].wait()

    def pick(k):
        yk = (y + k) % NY
        t_off = pl.multiple_of(yk * (NC * width_t), 128)
        s_off = pl.multiple_of(yk * (NC * width_s), 128)
        t_rows = jnp.dot(onehot, tb[:, pl.ds(t_off, NC * width_t)], preferred_element_type=F32)
        s_rows = jnp.dot(onehot, sb[:, pl.ds(s_off, NC * width_s)], preferred_element_type=F32)
        for h in range(NC):
            picked[k, h, :, :width_t] = t_rows[:, h * width_t : (h + 1) * width_t].astype(BF16)
            picked[k, h, :, width_t : width_t + width_s] = s_rows[:, h * width_s : (h + 1) * width_s].astype(BF16)

    pick(2)

    @pl.when(jnp.logical_not(clerk))
    def _():
        pl.semaphore_wait(barrier, NY * NC - 1)

    @pl.when(device(0, 1)[0] == CLERK)
    def _():
        pl.semaphore_signal(go, inc=1, device_id=device(0, 1), device_id_type=MESH)

    @pl.when(clerk)
    def _():
        pl.semaphore_wait(go, 1)

    sent = []
    arrived = {}

    def start(copy):
        copy.start()
        sent.append(copy)
        return copy

    for k in (2, 1, 3, 0):
        if k != 2:
            pick(k)
        for r in range(NC):
            if (k, r) != (0, 0):
                slot = slot_of(BACK[k], r)
                arrived[BACK[k], r] = start(remote(
                    picked.at[k, (c + r) % NC],
                    states.at[slot * TOK : (slot + 1) * TOK],
                    st_send.at[slot], st_recv.at[slot], device(k, r),
                ))
    states[:TOK] = picked[0, c]

    for dx, dz in [(0, dz) for dz in range(1, NZ)] + [(dx, 0) for dx in range(1, NX)]:
        there = (CLERK, device(0, 0, dx, dz)[1])
        pl.semaphore_signal(barrier, inc=1, device_id=there, device_id_type=MESH)

    def multiply(ks):
        first = min(PLACE[k] for k in ks) * PAIR
        rows = slice(first, first + len(ks) * PAIR)
        for m in range(2):
            if m == 0:
                part[m, rows] = jnp.dot(states[rows, :width_t], th[...], preferred_element_type=F32)
            else:
                part[m, rows] = jnp.dot(
                    states[rows, width_t : width_t + width_s], sh[...], preferred_element_type=F32
                )
            for k in ks:
                at = PLACE[k]
                sib_copies[m, k] = start(remote(
                    part.at[m, at * PAIR + TOK : (at + 1) * PAIR],
                    sib.at[m, at], sib_send.at[m, at], sib_recv.at[m, at], device(0, 1),
                ))

    def add_cores(m, k):
        sib_copies[m, k].wait_recv()
        at = PLACE[k]
        chip[m, at] = part[m, at * PAIR : at * PAIR + TOK] + sib[m, at]

    sib_copies = {}
    loads[3].wait()
    loads[4].wait()
    arrived[0, 1].wait_recv()
    multiply((0,))
    for r in range(NC):
        arrived[2, r].wait_recv()
    multiply((2,))
    for k in (1, 3):
        for r in range(NC):
            arrived[k, r].wait_recv()
    multiply((1, 3))

    opp_copies = []
    for m, k in ((0, 1), (1, 3)):
        add_cores(m, 2)
        opp_copies.append(start(remote(
            chip.at[m, PLACE[2]], opp.at[m], opp_send.at[m], opp_recv.at[m], device(k, 0)
        )))
    ring_copies = {}
    for m, k in ((1, 1), (0, 3)):
        add_cores(m, k)
        ring_copies[m, k] = start(remote(
            chip.at[m, PLACE[k]], ring.at[m, k // 2], ring_send.at[m, k // 2], ring_recv.at[m, k // 2], device(k, 0)
        ))
    for m, k in ((0, 1), (1, 3)):
        add_cores(m, k)
    for m, k in ((0, 1), (1, 3)):
        opp_copies[m].wait_recv()
        merged[m] = chip[m, PLACE[k]] + opp[m]
        ring_copies[m, k] = start(remote(
            merged.at[m], ring.at[m, k // 2], ring_send.at[m, k // 2], ring_recv.at[m, k // 2], device(k, 0)
        ))
    add_cores(0, 0)
    add_cores(1, 0)
    cols_ref[...] = jnp.transpose(states[:, width_t : width_t + width_s].astype(F32)).astype(BF16)

    for copy in ring_copies.values():
        copy.wait_recv()
    t_log = chip[0, 0] + (ring[0, 0] + ring[0, 1])
    s_log = chip[1, 0] + (ring[1, 0] + ring[1, 1])
    logits[0, 0] = t_log
    logits[0, 1] = s_log

    top_t = jnp.max(t_log, axis=1, keepdims=True)
    top_s = jnp.max(s_log, axis=1, keepdims=True)
    exp_t = jnp.exp(t_log - top_t)
    exp_s = jnp.exp(s_log - top_s)
    columns = [
        jnp.sum(exp_t, axis=1, keepdims=True),
        jnp.sum(exp_t * t_log, axis=1, keepdims=True),
        jnp.sum(exp_t * s_log, axis=1, keepdims=True),
        jnp.sum(exp_s, axis=1, keepdims=True),
        top_t, top_t, top_t, top_s,
    ]
    sub = lax.broadcasted_iota(jnp.int32, (TOK, 128), 0)
    lane = lax.broadcasted_iota(jnp.int32, (TOK, 128), 1)
    packed = jnp.zeros((TOK, 128), F32)
    for k, value in enumerate(columns):
        packed = jnp.where(lane == sub + k * TOK, value, packed)
    zbuf[0:1] = jnp.sum(packed, axis=0, keepdims=True)

    @pl.when(clerk)
    def _():
        pl.semaphore_wait(barrier, NY * NC * (NZ - 1 + NX - 1))
        for k, r in ((2, 0), (2, 1), (1, 0), (1, 1), (3, 0), (3, 1), (0, 1)):
            pl.semaphore_signal(far, inc=1, device_id=device(k, r), device_id_type=MESH)

    @pl.when(jnp.logical_not(clerk))
    def _():
        pl.semaphore_wait(far, 1)

    for dz in sorted(range(1, NZ), key=lambda d: -min(d, NZ - d)):
        remote(zbuf.at[0:1], zbuf.at[NZ - dz : NZ - dz + 1], z_sem.at[0], z_sem.at[1], device(0, 0, 0, dz)).start()

    def pass_logits(m, source, slot, target):
        start(remote(logits.at[source, m], logits.at[slot, m], lg_send.at[slot, m], lg_recv.at[slot, m], target))

    def arrive(m, k, r):
        slot = slot_of(k, r)
        landed = logits.at[slot, m]
        pltpu.make_async_copy(landed, landed, lg_recv.at[slot, m]).wait()
        if r == 0:
            if (m, k) == (0, 3):
                pass_logits(m, slot, slot_of(2, 0), device(1, 0))
            if (m, k) == (1, 1):
                pass_logits(m, slot, slot_of(2, 0), device(3, 0))
            pass_logits(m, slot, slot_of(k, 1), device(0, 1))

    def exponents(m, k, r):
        slot = slot_of(k, r)
        values = logits[slot, m]
        top = jnp.max(values, axis=1, keepdims=True)
        shifted[slot, m] = jnp.exp(values - top)
        tops[slot, m] = jnp.broadcast_to(top, (TOK, 128))

    for m, k in ((0, 1), (1, 3), (1, 1), (0, 3)):
        pass_logits(m, 0, slot_of(BACK[k], 0), device(k, 0))
    for m in range(2):
        pass_logits(m, 0, slot_of(0, 1), device(0, 1))

    shifted[0, 0] = exp_t
    shifted[0, 1] = exp_s
    tops[0, 0] = jnp.broadcast_to(top_t, (TOK, 128))
    tops[0, 1] = jnp.broadcast_to(top_s, (TOK, 128))
    for m in range(2):
        arrive(m, 0, 1)
        exponents(m, 0, 1)
    for m, k in ((0, 3), (1, 1), (1, 3), (0, 1)):
        arrive(m, k, 0)
    for m, k in ((0, 3), (1, 1), (1, 3), (0, 1)):
        exponents(m, k, 0)

    pltpu.make_async_copy(zbuf.at[1:NZ], zbuf.at[1:NZ], z_sem.at[1]).wait()
    pbuf[0:1] = combine(zbuf[...].reshape(NZ, 1, 128))
    plane = [(dx, k, r) for dx in (2, 1, 3, 0) for k in (2, 1, 3, 0) for r in range(NC) if (dx, k, r) != (0, 0, 0)]
    for dx, k, r in plane:
        row = BACK[dx] * NY * NC + slot_of(BACK[k], r)
        remote(pbuf.at[0:1], pbuf.at[row : row + 1], p_sem.at[0], p_sem.at[1], device(k, r, dx)).start()

    for m in range(2):
        arrive(m, 2, 0)
    for m, k in ((0, 3), (1, 1), (1, 3), (0, 1)):
        arrive(m, k, 1)
        exponents(m, k, 1)
    for m in range(2):
        exponents(m, 2, 0)
    for m in range(2):
        arrive(m, 2, 1)
        exponents(m, 2, 1)

    everyone = pbuf.at[1 : NX * NY * NC]
    pltpu.make_async_copy(everyone, everyone, p_sem.at[1]).wait()
    rows = combine(pbuf[...].reshape(NX, NY * NC, 128))

    sum_t = rows
    t_lse = lanes(rows, 4 * TOK) + jnp.log(sum_t)
    s_lse = lanes(rows, 7 * TOK) + jnp.log(lanes(rows, 3 * TOK))
    entropy = t_lse - lanes(rows, TOK) / sum_t
    weight = jnp.exp(-2.0 * entropy / math.log(vocab))
    loss_ref[...] = (weight * (s_lse - lanes(rows, 2 * TOK) / sum_t - entropy))[0:1]

    lane = lax.broadcasted_iota(jnp.int32, (NY * NC, TOK, 128), 2)
    sub = lax.broadcasted_iota(jnp.int32, (NY * NC, TOK, 128), 1)

    def column_of(values):
        spread = jnp.broadcast_to(values[:, None, :], (NY * NC, TOK, 128))
        return jnp.sum(jnp.where(lane == sub, spread, 0.0), axis=2, keepdims=True)

    scale = column_of(vocab / TOK * weight)
    scale_t = scale * jnp.exp(tops[:, 0] - column_of(t_lse))
    scale_s = scale * jnp.exp(tops[:, 1] - column_of(s_lse))
    for slot in range(NY * NC):
        grad = scale_s[slot, :, 0:1] * shifted[slot, 1] - scale_t[slot, :, 0:1] * shifted[slot, 0]
        grad_ref[slot * TOK : (slot + 1) * TOK] = grad.astype(BF16)

    for copy in sent:
        copy.wait_send()
    pltpu.make_async_copy(zbuf.at[1:NZ], zbuf.at[1:NZ], z_sem.at[0]).wait()
    pltpu.make_async_copy(everyone, everyone, p_sem.at[0]).wait()


def final_kernel(cols_ref, grad_ref, loss_in, head_ref, loss_ref):
    head_ref[...] = jnp.dot(cols_ref[...], grad_ref[...], preferred_element_type=F32).astype(BF16)
    loss_ref[...] = loss_in[:, :TOK]


def on_device(teacher_batch, student_batch, positions, teacher_head, student_head):
    width_t, shard = teacher_head.shape
    width_s = student_head.shape[0]
    vocab = shard * NX * NZ
    wide = 128 * pl.cdiv(width_t + width_s, 128)
    groups = NY * NC
    hbm = pl.BlockSpec(memory_space=pltpu.HBM)
    in_hbm = functools.partial(pltpu.with_memory_space_constraint, memory_space=pltpu.HBM)
    vmem = pl.BlockSpec(memory_space=pltpu.VMEM)
    dma = pltpu.SemaphoreType.DMA
    grad, cols, loss = pl.pallas_call(
        functools.partial(exchange_kernel, vocab, width_t, width_s, shard),
        out_shape=(
            pltpu.VMEM((ROWS, shard), BF16),
            pltpu.VMEM((width_s, ROWS), BF16),
            pltpu.VMEM((1, 128), F32),
        ),
        in_specs=[hbm] * 5,
        out_specs=(vmem, vmem, vmem),
        scratch_shapes=[
            pltpu.VMEM(teacher_batch.shape, BF16),
            pltpu.VMEM(student_batch.shape, BF16),
            pltpu.VMEM((1, TOK), jnp.int32),
            pltpu.VMEM(teacher_head.shape, BF16),
            pltpu.VMEM(student_head.shape, BF16),
            pltpu.VMEM((NY, NC, TOK, wide), BF16),
            pltpu.VMEM((ROWS, wide), BF16),
            pltpu.VMEM((2, ROWS, shard), F32),
            pltpu.VMEM((2, NY, TOK, shard), F32),
            pltpu.VMEM((2, NY, TOK, shard), F32),
            pltpu.VMEM((2, TOK, shard), F32),
            pltpu.VMEM((2, TOK, shard), F32),
            pltpu.VMEM((2, 2, TOK, shard), F32),
            pltpu.VMEM((groups, 2, TOK, shard), F32),
            pltpu.VMEM((groups, 2, TOK, shard), F32),
            pltpu.VMEM((groups, 2, TOK, 128), F32),
            pltpu.VMEM((NZ, 128), F32),
            pltpu.VMEM((NX * groups, 128), F32),
            dma((5,)),
            dma((groups,)), dma((groups,)),
            dma((2, NY)), dma((2, NY)),
            dma((2,)), dma((2,)),
            dma((2, 2)), dma((2, 2)),
            dma((groups, 2)), dma((groups, 2)),
            dma((2,)), dma((2,)),
            pltpu.SemaphoreType.REGULAR,
            pltpu.SemaphoreType.REGULAR,
        ],
        compiler_params=pltpu.CompilerParams(
            collective_id=0, has_side_effects=True, vmem_limit_bytes=32 * 1024 * 1024
        ),
    )(*map(in_hbm, (teacher_batch, student_batch, positions.reshape(1, TOK), teacher_head, student_head)))
    head_grad, loss = pl.pallas_call(
        final_kernel,
        out_shape=(
            jax.ShapeDtypeStruct((width_s, shard), BF16),
            jax.ShapeDtypeStruct((1, TOK), F32),
        ),
        in_specs=[vmem] * 3,
        out_specs=(vmem, vmem),
        compiler_params=pltpu.CompilerParams(vmem_limit_bytes=16 * 1024 * 1024),
    )(cols, grad, loss)
    return head_grad, loss.reshape(TOK)


def solution(mesh):
    in_specs = (P("tok", None), P("tok", None), P("tok"), P("tok", "voc"), P("tok", "voc"))
    out_specs = (P("tok", "voc"), P("tok"))
    return jax.shard_map(
        on_device, mesh=mesh, in_specs=in_specs, out_specs=out_specs, check_vma=False
    )
```

```python
import functools
import math

import jax
import jax.numpy as jnp
from jax import lax
from jax.experimental import pallas as pl
from jax.experimental.pallas import tpu as pltpu
from jax.sharding import PartitionSpec as P

MESH = pl.DeviceIdType.MESH
F32 = jnp.float32
BF16 = jnp.bfloat16
NY, NC, NX, NZ = 4, 2, 4, 16
TOK = 16
CLERK = 4
PAIR = NC * TOK
ROWS = NY * PAIR
PLACE = {0: 0, 1: 1, 3: 2, 2: 3}
BACK = {0: 0, 1: 3, 2: 2, 3: 1}


def slot_of(k, r):
    return PLACE[k] * NC + r


def remote(src, dst, send, recv, target):
    return pltpu.make_async_remote_copy(
        src_ref=src, dst_ref=dst, send_sem=send, recv_sem=recv, device_id=target, device_id_type=MESH
    )


def lanes(values, start):
    return pltpu.roll(values, (128 - start) % 128, axis=values.ndim - 1) if start else values


def combine(rows):
    tops = pltpu.roll(rows, 64, axis=2)
    top = jnp.max(tops, axis=0)
    total = jnp.sum(rows * jnp.exp(tops - top[None]), axis=0)
    lane = lax.broadcasted_iota(jnp.int32, total.shape, 1)
    return jnp.where(lane < 64, total, pltpu.roll(top, 64, axis=1))


def exchange_kernel(
    vocab, width_t, width_s, shard,
    tb_hbm, sb_hbm, pos_hbm, th_hbm, sh_hbm,
    grad_ref, cols_ref, loss_ref,
    tb, sb, pos, th, sh, picked, states, part, sib, chip, opp, merged, ring, logits, shifted, tops, zbuf, pbuf,
    load_sem, st_send, st_recv, sib_send, sib_recv, opp_send, opp_recv, ring_send, ring_recv,
    lg_send, lg_recv, z_sem, p_sem, go, far,
):
    tok, voc = lax.axis_index("tok"), lax.axis_index("voc")
    y, c = tok // NC, tok % NC
    z, x = voc // NX, voc % NX

    def device(k, r, dx=0, dz=0):
        return (((y + k) % NY) * NC + (c + r) % NC, ((z + dz) % NZ) * NX + (x + dx) % NX)

    loads = [
        pltpu.make_async_copy(src, dst, load_sem.at[i])
        for i, (src, dst) in enumerate(((pos_hbm, pos), (tb_hbm, tb), (sb_hbm, sb), (th_hbm, th), (sh_hbm, sh)))
    ]
    for load in loads[:3]:
        load.start()

    barrier = pltpu.get_barrier_semaphore()
    clerk = tok == CLERK
    for k, r in ((2, 0), (2, 1), (1, 0), (1, 1), (3, 0), (3, 1), (0, 1)):
        @pl.when(device(k, r)[0] != CLERK)
        def _():
            pl.semaphore_signal(barrier, inc=1, device_id=device(k, r), device_id_type=MESH)

    for load in loads[3:]:
        load.start()

    loads[0].wait()
    sub = lax.broadcasted_iota(jnp.int32, (TOK, TOK), 0)
    lane = lax.broadcasted_iota(jnp.int32, (TOK, TOK), 1)
    spread = jnp.where(sub == lane, jnp.broadcast_to(pos[...], (TOK, TOK)), 0).astype(F32)
    column = jnp.sum(spread, axis=1, keepdims=True).astype(jnp.int32)
    onehot = (lax.broadcasted_iota(jnp.int32, (TOK, tb.shape[0]), 1) == column).astype(BF16)
    loads[1].wait()
    loads[2].wait()

    def pick(k):
        yk = (y + k) % NY
        t_off = pl.multiple_of(yk * (NC * width_t), 128)
        s_off = pl.multiple_of(yk * (NC * width_s), 128)
        t_rows = jnp.dot(onehot, tb[:, pl.ds(t_off, NC * width_t)], preferred_element_type=F32)
        s_rows = jnp.dot(onehot, sb[:, pl.ds(s_off, NC * width_s)], preferred_element_type=F32)
        for h in range(NC):
            picked[k, h, :, :width_t] = t_rows[:, h * width_t : (h + 1) * width_t].astype(BF16)
            picked[k, h, :, width_t : width_t + width_s] = s_rows[:, h * width_s : (h + 1) * width_s].astype(BF16)

    pick(2)

    @pl.when(jnp.logical_not(clerk))
    def _():
        pl.semaphore_wait(barrier, NY * NC - 1)

    @pl.when(device(0, 1)[0] == CLERK)
    def _():
        pl.semaphore_signal(go, inc=1, device_id=device(0, 1), device_id_type=MESH)

    @pl.when(clerk)
    def _():
        pl.semaphore_wait(go, 1)

    sent = []
    arrived = {}

    def start(copy):
        copy.start()
        sent.append(copy)
        return copy

    for k in (2, 1, 3, 0):
        if k != 2:
            pick(k)
        for r in range(NC):
            if (k, r) != (0, 0):
                slot = slot_of(BACK[k], r)
                arrived[BACK[k], r] = start(remote(
                    picked.at[k, (c + r) % NC],
                    states.at[slot * TOK : (slot + 1) * TOK],
                    st_send.at[slot], st_recv.at[slot], device(k, r),
                ))
    states[:TOK] = picked[0, c]

    for dx, dz in [(0, dz) for dz in range(1, NZ)] + [(dx, 0) for dx in range(1, NX)]:
        there = (CLERK, device(0, 0, dx, dz)[1])
        pl.semaphore_signal(barrier, inc=1, device_id=there, device_id_type=MESH)

    def multiply(ks):
        first = min(PLACE[k] for k in ks) * PAIR
        rows = slice(first, first + len(ks) * PAIR)
        for m in range(2):
            if m == 0:
                part[m, rows] = jnp.dot(states[rows, :width_t], th[...], preferred_element_type=F32)
            else:
                part[m, rows] = jnp.dot(
                    states[rows, width_t : width_t + width_s], sh[...], preferred_element_type=F32
                )
            for k in ks:
                at = PLACE[k]
                sib_copies[m, k] = start(remote(
                    part.at[m, at * PAIR + TOK : (at + 1) * PAIR],
                    sib.at[m, at], sib_send.at[m, at], sib_recv.at[m, at], device(0, 1),
                ))

    def add_cores(m, k):
        sib_copies[m, k].wait_recv()
        at = PLACE[k]
        chip[m, at] = part[m, at * PAIR : at * PAIR + TOK] + sib[m, at]

    sib_copies = {}
    loads[3].wait()
    loads[4].wait()
    arrived[0, 1].wait_recv()
    multiply((0,))
    for r in range(NC):
        arrived[2, r].wait_recv()
    multiply((2,))

    opp_copies = []
    for m, k in ((0, 1), (1, 3)):
        add_cores(m, 2)
        opp_copies.append(start(remote(
            chip.at[m, PLACE[2]], opp.at[m], opp_send.at[m], opp_recv.at[m], device(k, 0)
        )))
    for k in (1, 3):
        for r in range(NC):
            arrived[k, r].wait_recv()
    multiply((1, 3))
    ring_copies = {}
    for m, k in ((1, 1), (0, 3)):
        add_cores(m, k)
        ring_copies[m, k] = start(remote(
            chip.at[m, PLACE[k]], ring.at[m, k // 2], ring_send.at[m, k // 2], ring_recv.at[m, k // 2], device(k, 0)
        ))
    for m, k in ((0, 1), (1, 3)):
        add_cores(m, k)
    for m, k in ((0, 1), (1, 3)):
        opp_copies[m].wait_recv()
        merged[m] = chip[m, PLACE[k]] + opp[m]
        ring_copies[m, k] = start(remote(
            merged.at[m], ring.at[m, k // 2], ring_send.at[m, k // 2], ring_recv.at[m, k // 2], device(k, 0)
        ))
    @pl.when(clerk)
    def _():
        pl.semaphore_wait(barrier, NY * NC * (NZ - 1 + NX - 1))
        for k, r in ((2, 0), (2, 1), (1, 0), (1, 1), (3, 0), (3, 1), (0, 1)):
            pl.semaphore_signal(far, inc=1, device_id=device(k, r), device_id_type=MESH)

    add_cores(0, 0)
    add_cores(1, 0)
    cols_ref[...] = jnp.transpose(states[:, width_t : width_t + width_s].astype(F32)).astype(BF16)

    for copy in ring_copies.values():
        copy.wait_recv()
    t_log = chip[0, 0] + (ring[0, 0] + ring[0, 1])
    s_log = chip[1, 0] + (ring[1, 0] + ring[1, 1])
    logits[0, 0] = t_log
    logits[0, 1] = s_log

    top_t = jnp.max(t_log, axis=1, keepdims=True)
    top_s = jnp.max(s_log, axis=1, keepdims=True)
    exp_t = jnp.exp(t_log - top_t)
    exp_s = jnp.exp(s_log - top_s)
    columns = [
        jnp.sum(exp_t, axis=1, keepdims=True),
        jnp.sum(exp_t * t_log, axis=1, keepdims=True),
        jnp.sum(exp_t * s_log, axis=1, keepdims=True),
        jnp.sum(exp_s, axis=1, keepdims=True),
        top_t, top_t, top_t, top_s,
    ]
    sub = lax.broadcasted_iota(jnp.int32, (TOK, 128), 0)
    lane = lax.broadcasted_iota(jnp.int32, (TOK, 128), 1)
    packed = jnp.zeros((TOK, 128), F32)
    for k, value in enumerate(columns):
        packed = jnp.where(lane == sub + k * TOK, value, packed)
    zbuf[0:1] = jnp.sum(packed, axis=0, keepdims=True)

    @pl.when(jnp.logical_not(clerk))
    def _():
        pl.semaphore_wait(far, 1)

    for dz in sorted(range(1, NZ), key=lambda d: -min(d, NZ - d)):
        remote(zbuf.at[0:1], zbuf.at[NZ - dz : NZ - dz + 1], z_sem.at[0], z_sem.at[1], device(0, 0, 0, dz)).start()

    def pass_logits(m, source, slot, target):
        start(remote(logits.at[source, m], logits.at[slot, m], lg_send.at[slot, m], lg_recv.at[slot, m], target))

    def arrive(m, k, r):
        slot = slot_of(k, r)
        landed = logits.at[slot, m]
        pltpu.make_async_copy(landed, landed, lg_recv.at[slot, m]).wait()
        if r == 0:
            if (m, k) == (0, 3):
                pass_logits(m, slot, slot_of(2, 0), device(1, 0))
            if (m, k) == (1, 1):
                pass_logits(m, slot, slot_of(2, 0), device(3, 0))
            pass_logits(m, slot, slot_of(k, 1), device(0, 1))

    def exponents(m, k, r):
        slot = slot_of(k, r)
        values = logits[slot, m]
        top = jnp.max(values, axis=1, keepdims=True)
        shifted[slot, m] = jnp.exp(values - top)
        tops[slot, m] = jnp.broadcast_to(top, (TOK, 128))

    for m, k in ((0, 1), (1, 3), (1, 1), (0, 3)):
        pass_logits(m, 0, slot_of(BACK[k], 0), device(k, 0))
    for m in range(2):
        pass_logits(m, 0, slot_of(0, 1), device(0, 1))

    shifted[0, 0] = exp_t
    shifted[0, 1] = exp_s
    tops[0, 0] = jnp.broadcast_to(top_t, (TOK, 128))
    tops[0, 1] = jnp.broadcast_to(top_s, (TOK, 128))
    for m in range(2):
        arrive(m, 0, 1)
        exponents(m, 0, 1)
    for m, k in ((0, 3), (1, 1), (1, 3), (0, 1)):
        arrive(m, k, 0)
    for m, k in ((0, 3), (1, 1), (1, 3), (0, 1)):
        exponents(m, k, 0)

    pltpu.make_async_copy(zbuf.at[1:NZ], zbuf.at[1:NZ], z_sem.at[1]).wait()
    pbuf[0:1] = combine(zbuf[...].reshape(NZ, 1, 128))
    plane = [(dx, k, r) for dx in (2, 1, 3, 0) for k in (2, 1, 3, 0) for r in range(NC) if (dx, k, r) != (0, 0, 0)]
    for dx, k, r in plane:
        row = BACK[dx] * NY * NC + slot_of(BACK[k], r)
        remote(pbuf.at[0:1], pbuf.at[row : row + 1], p_sem.at[0], p_sem.at[1], device(k, r, dx)).start()

    for m in range(2):
        arrive(m, 2, 0)
    for m, k in ((0, 3), (1, 1), (1, 3), (0, 1)):
        arrive(m, k, 1)
        exponents(m, k, 1)
    for m in range(2):
        exponents(m, 2, 0)
    for m in range(2):
        arrive(m, 2, 1)
        exponents(m, 2, 1)

    everyone = pbuf.at[1 : NX * NY * NC]
    pltpu.make_async_copy(everyone, everyone, p_sem.at[1]).wait()
    rows = combine(pbuf[...].reshape(NX, NY * NC, 128))

    sum_t = rows
    t_lse = lanes(rows, 4 * TOK) + jnp.log(sum_t)
    s_lse = lanes(rows, 7 * TOK) + jnp.log(lanes(rows, 3 * TOK))
    entropy = t_lse - lanes(rows, TOK) / sum_t
    weight = jnp.exp(-2.0 * entropy / math.log(vocab))
    loss_ref[...] = (weight * (s_lse - lanes(rows, 2 * TOK) / sum_t - entropy))[0:1]

    lane = lax.broadcasted_iota(jnp.int32, (NY * NC, TOK, 128), 2)
    sub = lax.broadcasted_iota(jnp.int32, (NY * NC, TOK, 128), 1)

    def column_of(values):
        spread = jnp.broadcast_to(values[:, None, :], (NY * NC, TOK, 128))
        return jnp.sum(jnp.where(lane == sub, spread, 0.0), axis=2, keepdims=True)

    scale = column_of(vocab / TOK * weight)
    scale_t = scale * jnp.exp(tops[:, 0] - column_of(t_lse))
    scale_s = scale * jnp.exp(tops[:, 1] - column_of(s_lse))
    for slot in range(NY * NC):
        grad = scale_s[slot, :, 0:1] * shifted[slot, 1] - scale_t[slot, :, 0:1] * shifted[slot, 0]
        grad_ref[slot * TOK : (slot + 1) * TOK] = grad.astype(BF16)

    for copy in sent:
        copy.wait_send()
    pltpu.make_async_copy(zbuf.at[1:NZ], zbuf.at[1:NZ], z_sem.at[0]).wait()
    pltpu.make_async_copy(everyone, everyone, p_sem.at[0]).wait()


def final_kernel(cols_ref, grad_ref, loss_in, head_ref, loss_ref):
    head_ref[...] = jnp.dot(cols_ref[...], grad_ref[...], preferred_element_type=F32).astype(BF16)
    loss_ref[...] = loss_in[:, :TOK]


def on_device(teacher_batch, student_batch, positions, teacher_head, student_head):
    width_t, shard = teacher_head.shape
    width_s = student_head.shape[0]
    vocab = shard * NX * NZ
    wide = 128 * pl.cdiv(width_t + width_s, 128)
    groups = NY * NC
    hbm = pl.BlockSpec(memory_space=pltpu.HBM)
    in_hbm = functools.partial(pltpu.with_memory_space_constraint, memory_space=pltpu.HBM)
    vmem = pl.BlockSpec(memory_space=pltpu.VMEM)
    dma = pltpu.SemaphoreType.DMA
    grad, cols, loss = pl.pallas_call(
        functools.partial(exchange_kernel, vocab, width_t, width_s, shard),
        out_shape=(
            pltpu.VMEM((ROWS, shard), BF16),
            pltpu.VMEM((width_s, ROWS), BF16),
            pltpu.VMEM((1, 128), F32),
        ),
        in_specs=[hbm] * 5,
        out_specs=(vmem, vmem, vmem),
        scratch_shapes=[
            pltpu.VMEM(teacher_batch.shape, BF16),
            pltpu.VMEM(student_batch.shape, BF16),
            pltpu.VMEM((1, TOK), jnp.int32),
            pltpu.VMEM(teacher_head.shape, BF16),
            pltpu.VMEM(student_head.shape, BF16),
            pltpu.VMEM((NY, NC, TOK, wide), BF16),
            pltpu.VMEM((ROWS, wide), BF16),
            pltpu.VMEM((2, ROWS, shard), F32),
            pltpu.VMEM((2, NY, TOK, shard), F32),
            pltpu.VMEM((2, NY, TOK, shard), F32),
            pltpu.VMEM((2, TOK, shard), F32),
            pltpu.VMEM((2, TOK, shard), F32),
            pltpu.VMEM((2, 2, TOK, shard), F32),
            pltpu.VMEM((groups, 2, TOK, shard), F32),
            pltpu.VMEM((groups, 2, TOK, shard), F32),
            pltpu.VMEM((groups, 2, TOK, 128), F32),
            pltpu.VMEM((NZ, 128), F32),
            pltpu.VMEM((NX * groups, 128), F32),
            dma((5,)),
            dma((groups,)), dma((groups,)),
            dma((2, NY)), dma((2, NY)),
            dma((2,)), dma((2,)),
            dma((2, 2)), dma((2, 2)),
            dma((groups, 2)), dma((groups, 2)),
            dma((2,)), dma((2,)),
            pltpu.SemaphoreType.REGULAR,
            pltpu.SemaphoreType.REGULAR,
        ],
        compiler_params=pltpu.CompilerParams(
            collective_id=0, has_side_effects=True, vmem_limit_bytes=32 * 1024 * 1024
        ),
    )(*map(in_hbm, (teacher_batch, student_batch, positions.reshape(1, TOK), teacher_head, student_head)))
    head_grad, loss = pl.pallas_call(
        final_kernel,
        out_shape=(
            jax.ShapeDtypeStruct((width_s, shard), BF16),
            jax.ShapeDtypeStruct((1, TOK), F32),
        ),
        in_specs=[vmem] * 3,
        out_specs=(vmem, vmem),
        compiler_params=pltpu.CompilerParams(vmem_limit_bytes=16 * 1024 * 1024),
    )(cols, grad, loss)
    return head_grad, loss.reshape(TOK)


def solution(mesh):
    in_specs = (P("tok", None), P("tok", None), P("tok"), P("tok", "voc"), P("tok", "voc"))
    out_specs = (P("tok", "voc"), P("tok"))
    return jax.shard_map(
        on_device, mesh=mesh, in_specs=in_specs, out_specs=out_specs, check_vma=False
    )
```

```python
import functools
import math

import jax
import jax.numpy as jnp
from jax import lax
from jax.experimental import pallas as pl
from jax.experimental.pallas import tpu as pltpu
from jax.sharding import PartitionSpec as P

MESH = pl.DeviceIdType.MESH
F32 = jnp.float32
BF16 = jnp.bfloat16
NY, NC, NX, NZ = 4, 2, 4, 16
TOK = 16
CLERK = 4
PAIR = NC * TOK
ROWS = NY * PAIR
PLACE = {0: 0, 1: 1, 3: 2, 2: 3}
BACK = {0: 0, 1: 3, 2: 2, 3: 1}


def slot_of(k, r):
    return PLACE[k] * NC + r


def remote(src, dst, send, recv, target):
    return pltpu.make_async_remote_copy(
        src_ref=src, dst_ref=dst, send_sem=send, recv_sem=recv, device_id=target, device_id_type=MESH
    )


def lanes(values, start):
    return pltpu.roll(values, (128 - start) % 128, axis=values.ndim - 1) if start else values


def combine(rows):
    tops = pltpu.roll(rows, 64, axis=2)
    top = jnp.max(tops, axis=0)
    total = jnp.sum(rows * jnp.exp(tops - top[None]), axis=0)
    lane = lax.broadcasted_iota(jnp.int32, total.shape, 1)
    return jnp.where(lane < 64, total, pltpu.roll(top, 64, axis=1))


def exchange_kernel(
    vocab, width_t, width_s, shard,
    tb_hbm, sb_hbm, pos_hbm, th_hbm, sh_hbm,
    grad_ref, cols_ref, loss_ref,
    tb, sb, pos, th, sh, picked, states, part, sib, chip, opp, merged, ring, logits, shifted, tops, zbuf, pbuf,
    load_sem, st_send, st_recv, sib_send, sib_recv, opp_send, opp_recv, ring_send, ring_recv,
    lg_send, lg_recv, z_sem, p_sem, go, far,
):
    tok, voc = lax.axis_index("tok"), lax.axis_index("voc")
    y, c = tok // NC, tok % NC
    z, x = voc // NX, voc % NX

    def device(k, r, dx=0, dz=0):
        return (((y + k) % NY) * NC + (c + r) % NC, ((z + dz) % NZ) * NX + (x + dx) % NX)

    loads = [
        pltpu.make_async_copy(src, dst, load_sem.at[i])
        for i, (src, dst) in enumerate(((pos_hbm, pos), (tb_hbm, tb), (sb_hbm, sb), (th_hbm, th), (sh_hbm, sh)))
    ]
    barrier = pltpu.get_barrier_semaphore()
    clerk = tok == CLERK
    for k, r in ((2, 0), (2, 1), (1, 0), (1, 1), (3, 0), (3, 1), (0, 1)):
        @pl.when(device(k, r)[0] != CLERK)
        def _():
            pl.semaphore_signal(barrier, inc=1, device_id=device(k, r), device_id_type=MESH)

    for load in loads:
        load.start()

    loads[0].wait()
    sub = lax.broadcasted_iota(jnp.int32, (TOK, TOK), 0)
    lane = lax.broadcasted_iota(jnp.int32, (TOK, TOK), 1)
    spread = jnp.where(sub == lane, jnp.broadcast_to(pos[...], (TOK, TOK)), 0).astype(F32)
    column = jnp.sum(spread, axis=1, keepdims=True).astype(jnp.int32)
    onehot = (lax.broadcasted_iota(jnp.int32, (TOK, tb.shape[0]), 1) == column).astype(BF16)
    loads[1].wait()
    loads[2].wait()

    def pick(k):
        yk = (y + k) % NY
        t_off = pl.multiple_of(yk * (NC * width_t), 128)
        s_off = pl.multiple_of(yk * (NC * width_s), 128)
        t_rows = jnp.dot(onehot, tb[:, pl.ds(t_off, NC * width_t)], preferred_element_type=F32)
        s_rows = jnp.dot(onehot, sb[:, pl.ds(s_off, NC * width_s)], preferred_element_type=F32)
        for h in range(NC):
            picked[k, h, :, :width_t] = t_rows[:, h * width_t : (h + 1) * width_t].astype(BF16)
            picked[k, h, :, width_t : width_t + width_s] = s_rows[:, h * width_s : (h + 1) * width_s].astype(BF16)

    pick(2)

    @pl.when(jnp.logical_not(clerk))
    def _():
        pl.semaphore_wait(barrier, NY * NC - 1)

    @pl.when(device(0, 1)[0] == CLERK)
    def _():
        pl.semaphore_signal(go, inc=1, device_id=device(0, 1), device_id_type=MESH)

    @pl.when(clerk)
    def _():
        pl.semaphore_wait(go, 1)

    sent = []
    arrived = {}

    def start(copy):
        copy.start()
        sent.append(copy)
        return copy

    for k in (2, 1, 3, 0):
        if k != 2:
            pick(k)
        for r in range(NC):
            if (k, r) != (0, 0):
                slot = slot_of(BACK[k], r)
                arrived[BACK[k], r] = start(remote(
                    picked.at[k, (c + r) % NC],
                    states.at[slot * TOK : (slot + 1) * TOK],
                    st_send.at[slot], st_recv.at[slot], device(k, r),
                ))
    states[:TOK] = picked[0, c]

    for dx, dz in [(0, dz) for dz in range(1, NZ)] + [(dx, 0) for dx in range(1, NX)]:
        there = (CLERK, device(0, 0, dx, dz)[1])
        pl.semaphore_signal(barrier, inc=1, device_id=there, device_id_type=MESH)

    def multiply(ks):
        first = min(PLACE[k] for k in ks) * PAIR
        rows = slice(first, first + len(ks) * PAIR)
        for m in range(2):
            if m == 0:
                part[m, rows] = jnp.dot(states[rows, :width_t], th[...], preferred_element_type=F32)
            else:
                part[m, rows] = jnp.dot(
                    states[rows, width_t : width_t + width_s], sh[...], preferred_element_type=F32
                )
            for k in ks:
                at = PLACE[k]
                sib_copies[m, k] = start(remote(
                    part.at[m, at * PAIR + TOK : (at + 1) * PAIR],
                    sib.at[m, at], sib_send.at[m, at], sib_recv.at[m, at], device(0, 1),
                ))

    def add_cores(m, k):
        sib_copies[m, k].wait_recv()
        at = PLACE[k]
        chip[m, at] = part[m, at * PAIR : at * PAIR + TOK] + sib[m, at]

    sib_copies = {}
    loads[3].wait()
    loads[4].wait()
    arrived[0, 1].wait_recv()
    multiply((0,))
    for r in range(NC):
        arrived[2, r].wait_recv()
    multiply((2,))

    opp_copies = []
    for m, k in ((0, 1), (1, 3)):
        add_cores(m, 2)
        opp_copies.append(start(remote(
            chip.at[m, PLACE[2]], opp.at[m], opp_send.at[m], opp_recv.at[m], device(k, 0)
        )))
    for k in (1, 3):
        for r in range(NC):
            arrived[k, r].wait_recv()
    multiply((1, 3))
    ring_copies = {}
    for m, k in ((1, 1), (0, 3)):
        add_cores(m, k)
        ring_copies[m, k] = start(remote(
            chip.at[m, PLACE[k]], ring.at[m, k // 2], ring_send.at[m, k // 2], ring_recv.at[m, k // 2], device(k, 0)
        ))
    for m, k in ((0, 1), (1, 3)):
        add_cores(m, k)
    for m, k in ((0, 1), (1, 3)):
        opp_copies[m].wait_recv()
        merged[m] = chip[m, PLACE[k]] + opp[m]
        ring_copies[m, k] = start(remote(
            merged.at[m], ring.at[m, k // 2], ring_send.at[m, k // 2], ring_recv.at[m, k // 2], device(k, 0)
        ))
    @pl.when(clerk)
    def _():
        pl.semaphore_wait(barrier, NY * NC * (NZ - 1 + NX - 1))
        for k, r in ((2, 0), (2, 1), (1, 0), (1, 1), (3, 0), (3, 1), (0, 1)):
            pl.semaphore_signal(far, inc=1, device_id=device(k, r), device_id_type=MESH)

    add_cores(0, 0)
    add_cores(1, 0)
    cols_ref[...] = jnp.transpose(states[:, width_t : width_t + width_s].astype(F32)).astype(BF16)

    for copy in ring_copies.values():
        copy.wait_recv()
    t_log = chip[0, 0] + (ring[0, 0] + ring[0, 1])
    s_log = chip[1, 0] + (ring[1, 0] + ring[1, 1])
    logits[0, 0] = t_log
    logits[0, 1] = s_log

    top_t = jnp.max(t_log, axis=1, keepdims=True)
    top_s = jnp.max(s_log, axis=1, keepdims=True)
    exp_t = jnp.exp(t_log - top_t)
    exp_s = jnp.exp(s_log - top_s)
    columns = [
        jnp.sum(exp_t, axis=1, keepdims=True),
        jnp.sum(exp_t * t_log, axis=1, keepdims=True),
        jnp.sum(exp_t * s_log, axis=1, keepdims=True),
        jnp.sum(exp_s, axis=1, keepdims=True),
        top_t, top_t, top_t, top_s,
    ]
    sub = lax.broadcasted_iota(jnp.int32, (TOK, 128), 0)
    lane = lax.broadcasted_iota(jnp.int32, (TOK, 128), 1)
    packed = jnp.zeros((TOK, 128), F32)
    for k, value in enumerate(columns):
        packed = jnp.where(lane == sub + k * TOK, value, packed)
    zbuf[0:1] = jnp.sum(packed, axis=0, keepdims=True)

    @pl.when(jnp.logical_not(clerk))
    def _():
        pl.semaphore_wait(far, 1)

    for dz in sorted(range(1, NZ), key=lambda d: -min(d, NZ - d)):
        remote(zbuf.at[0:1], zbuf.at[NZ - dz : NZ - dz + 1], z_sem.at[0], z_sem.at[1], device(0, 0, 0, dz)).start()

    def pass_logits(m, source, slot, target):
        start(remote(logits.at[source, m], logits.at[slot, m], lg_send.at[slot, m], lg_recv.at[slot, m], target))

    def arrive(m, k, r):
        slot = slot_of(k, r)
        landed = logits.at[slot, m]
        pltpu.make_async_copy(landed, landed, lg_recv.at[slot, m]).wait()
        if r == 0:
            if (m, k) == (0, 3):
                pass_logits(m, slot, slot_of(2, 0), device(1, 0))
            if (m, k) == (1, 1):
                pass_logits(m, slot, slot_of(2, 0), device(3, 0))
            pass_logits(m, slot, slot_of(k, 1), device(0, 1))

    def exponents(m, k, r):
        slot = slot_of(k, r)
        values = logits[slot, m]
        top = jnp.max(values, axis=1, keepdims=True)
        shifted[slot, m] = jnp.exp(values - top)
        tops[slot, m] = jnp.broadcast_to(top, (TOK, 128))

    for m, k in ((0, 1), (1, 3), (1, 1), (0, 3)):
        pass_logits(m, 0, slot_of(BACK[k], 0), device(k, 0))
    for m in range(2):
        pass_logits(m, 0, slot_of(0, 1), device(0, 1))

    shifted[0, 0] = exp_t
    shifted[0, 1] = exp_s
    tops[0, 0] = jnp.broadcast_to(top_t, (TOK, 128))
    tops[0, 1] = jnp.broadcast_to(top_s, (TOK, 128))
    for m in range(2):
        arrive(m, 0, 1)
        exponents(m, 0, 1)
    for m, k in ((0, 3), (1, 1), (1, 3), (0, 1)):
        arrive(m, k, 0)
    for m, k in ((0, 3), (1, 1), (1, 3), (0, 1)):
        exponents(m, k, 0)

    pltpu.make_async_copy(zbuf.at[1:NZ], zbuf.at[1:NZ], z_sem.at[1]).wait()
    pbuf[0:1] = combine(zbuf[...].reshape(NZ, 1, 128))
    plane = [(dx, k, r) for dx in (2, 1, 3, 0) for k in (2, 1, 3, 0) for r in range(NC) if (dx, k, r) != (0, 0, 0)]
    for dx, k, r in plane:
        row = BACK[dx] * NY * NC + slot_of(BACK[k], r)
        remote(pbuf.at[0:1], pbuf.at[row : row + 1], p_sem.at[0], p_sem.at[1], device(k, r, dx)).start()

    for m in range(2):
        arrive(m, 2, 0)
    for m, k in ((0, 3), (1, 1), (1, 3), (0, 1)):
        arrive(m, k, 1)
        exponents(m, k, 1)
    for m in range(2):
        exponents(m, 2, 0)
    for m in range(2):
        arrive(m, 2, 1)
        exponents(m, 2, 1)

    everyone = pbuf.at[1 : NX * NY * NC]
    pltpu.make_async_copy(everyone, everyone, p_sem.at[1]).wait()
    rows = combine(pbuf[...].reshape(NX, NY * NC, 128))

    sum_t = rows
    t_lse = lanes(rows, 4 * TOK) + jnp.log(sum_t)
    s_lse = lanes(rows, 7 * TOK) + jnp.log(lanes(rows, 3 * TOK))
    entropy = t_lse - lanes(rows, TOK) / sum_t
    log_weight = entropy * (-2.0 / math.log(vocab))
    loss_ref[...] = (jnp.exp(log_weight) * (s_lse - lanes(rows, 2 * TOK) / sum_t - entropy))[0:1]
    log_scale = log_weight + math.log(vocab / TOK)

    lane = lax.broadcasted_iota(jnp.int32, (NY * NC, TOK, 128), 2)
    sub = lax.broadcasted_iota(jnp.int32, (NY * NC, TOK, 128), 1)

    def column_of(values):
        spread = jnp.broadcast_to(values[:, None, :], (NY * NC, TOK, 128))
        return jnp.sum(jnp.where(lane == sub, spread, 0.0), axis=2, keepdims=True)

    scale_t = jnp.exp(tops[:, 0] + column_of(log_scale - t_lse))
    scale_s = jnp.exp(tops[:, 1] + column_of(log_scale - s_lse))
    for slot in range(NY * NC):
        for at in range(0, shard, 128):
            cut = slice(at, at + 128)
            grad = scale_s[slot] * shifted[slot, 1, :, cut] - scale_t[slot] * shifted[slot, 0, :, cut]
            grad_ref[slot * TOK : (slot + 1) * TOK, cut] = grad.astype(BF16)

    for copy in sent:
        copy.wait_send()
    pltpu.make_async_copy(zbuf.at[1:NZ], zbuf.at[1:NZ], z_sem.at[0]).wait()
    pltpu.make_async_copy(everyone, everyone, p_sem.at[0]).wait()


def final_kernel(pieces, cols_ref, grad_ref, loss_in, head_hbm, loss_hbm, head, loss, sem):
    loss[...] = loss_in[:, :TOK]
    copies = [pltpu.make_async_copy(loss, loss_hbm, sem.at[pieces])]
    copies[0].start()
    tall = head.shape[0] // pieces
    for i in range(pieces):
        at = slice(i * tall, (i + 1) * tall)
        head[at] = jnp.dot(cols_ref[at], grad_ref[...], preferred_element_type=F32).astype(BF16)
        copies.append(pltpu.make_async_copy(head.at[at], head_hbm.at[at], sem.at[i]))
        copies[-1].start()
    for copy in copies:
        copy.wait()


def on_device(teacher_batch, student_batch, positions, teacher_head, student_head):
    width_t, shard = teacher_head.shape
    width_s = student_head.shape[0]
    vocab = shard * NX * NZ
    wide = 128 * pl.cdiv(width_t + width_s, 128)
    groups = NY * NC
    hbm = pl.BlockSpec(memory_space=pltpu.HBM)
    in_hbm = functools.partial(pltpu.with_memory_space_constraint, memory_space=pltpu.HBM)
    vmem = pl.BlockSpec(memory_space=pltpu.VMEM)
    dma = pltpu.SemaphoreType.DMA
    grad, cols, loss = pl.pallas_call(
        functools.partial(exchange_kernel, vocab, width_t, width_s, shard),
        out_shape=(
            pltpu.VMEM((ROWS, shard), BF16),
            pltpu.VMEM((width_s, ROWS), BF16),
            pltpu.VMEM((1, 128), F32),
        ),
        in_specs=[hbm] * 5,
        out_specs=(vmem, vmem, vmem),
        scratch_shapes=[
            pltpu.VMEM(teacher_batch.shape, BF16),
            pltpu.VMEM(student_batch.shape, BF16),
            pltpu.VMEM((1, TOK), jnp.int32),
            pltpu.VMEM(teacher_head.shape, BF16),
            pltpu.VMEM(student_head.shape, BF16),
            pltpu.VMEM((NY, NC, TOK, wide), BF16),
            pltpu.VMEM((ROWS, wide), BF16),
            pltpu.VMEM((2, ROWS, shard), F32),
            pltpu.VMEM((2, NY, TOK, shard), F32),
            pltpu.VMEM((2, NY, TOK, shard), F32),
            pltpu.VMEM((2, TOK, shard), F32),
            pltpu.VMEM((2, TOK, shard), F32),
            pltpu.VMEM((2, 2, TOK, shard), F32),
            pltpu.VMEM((groups, 2, TOK, shard), F32),
            pltpu.VMEM((groups, 2, TOK, shard), F32),
            pltpu.VMEM((groups, 2, TOK, 128), F32),
            pltpu.VMEM((NZ, 128), F32),
            pltpu.VMEM((NX * groups, 128), F32),
            dma((5,)),
            dma((groups,)), dma((groups,)),
            dma((2, NY)), dma((2, NY)),
            dma((2,)), dma((2,)),
            dma((2, 2)), dma((2, 2)),
            dma((groups, 2)), dma((groups, 2)),
            dma((2,)), dma((2,)),
            pltpu.SemaphoreType.REGULAR,
            pltpu.SemaphoreType.REGULAR,
        ],
        compiler_params=pltpu.CompilerParams(
            collective_id=0, has_side_effects=True, vmem_limit_bytes=32 * 1024 * 1024
        ),
    )(*map(in_hbm, (teacher_batch, student_batch, positions.reshape(1, TOK), teacher_head, student_head)))
    pieces = 4
    head_grad, loss = pl.pallas_call(
        functools.partial(final_kernel, pieces),
        out_shape=(
            jax.ShapeDtypeStruct((width_s, shard), BF16),
            jax.ShapeDtypeStruct((1, TOK), F32),
        ),
        in_specs=[vmem] * 3,
        out_specs=(hbm, hbm),
        scratch_shapes=[pltpu.VMEM((width_s, shard), BF16), pltpu.VMEM((1, TOK), F32), dma((pieces + 1,))],
        compiler_params=pltpu.CompilerParams(vmem_limit_bytes=16 * 1024 * 1024),
    )(cols, grad, loss)
    return head_grad, loss.reshape(TOK)


def solution(mesh):
    in_specs = (P("tok", None), P("tok", None), P("tok"), P("tok", "voc"), P("tok", "voc"))
    out_specs = (P("tok", "voc"), P("tok"))
    return jax.shard_map(
        on_device, mesh=mesh, in_specs=in_specs, out_specs=out_specs, check_vma=False
    )
```

```python
import functools
import math

import jax
import jax.numpy as jnp
from jax import lax
from jax.experimental import pallas as pl
from jax.experimental.pallas import tpu as pltpu
from jax.sharding import PartitionSpec as P

MESH = pl.DeviceIdType.MESH
F32 = jnp.float32
BF16 = jnp.bfloat16
NY, NC, NX, NZ = 4, 2, 4, 16
TOK = 16
CLERK = 4
PAIR = NC * TOK
ROWS = NY * PAIR
PLACE = {0: 0, 1: 1, 3: 2, 2: 3}
BACK = {0: 0, 1: 3, 2: 2, 3: 1}


def slot_of(k, r):
    return PLACE[k] * NC + r


def remote(src, dst, send, recv, target):
    return pltpu.make_async_remote_copy(
        src_ref=src, dst_ref=dst, send_sem=send, recv_sem=recv, device_id=target, device_id_type=MESH
    )


def lanes(values, start):
    return pltpu.roll(values, (128 - start) % 128, axis=values.ndim - 1) if start else values


def combine(rows):
    tops = pltpu.roll(rows, 64, axis=2)
    top = jnp.max(tops, axis=0)
    total = jnp.sum(rows * jnp.exp(tops - top[None]), axis=0)
    lane = lax.broadcasted_iota(jnp.int32, total.shape, 1)
    return jnp.where(lane < 64, total, pltpu.roll(top, 64, axis=1))


def exchange_kernel(
    vocab, width_t, width_s, shard,
    tb_hbm, sb_hbm, pos_hbm, th_hbm, sh_hbm,
    grad_ref, cols_ref, loss_ref,
    tb, sb, pos, th, sh, picked, states, part, sib, chip, opp, merged, ring, logits, shifted, tops, zbuf, pbuf,
    load_sem, st_send, st_recv, sib_send, sib_recv, opp_send, opp_recv, ring_send, ring_recv,
    lg_send, lg_recv, z_sem, p_sem, go, far,
):
    tok, voc = lax.axis_index("tok"), lax.axis_index("voc")
    y, c = tok // NC, tok % NC
    z, x = voc // NX, voc % NX

    def device(k, r, dx=0, dz=0):
        return (((y + k) % NY) * NC + (c + r) % NC, ((z + dz) % NZ) * NX + (x + dx) % NX)

    loads = [
        pltpu.make_async_copy(src, dst, load_sem.at[i])
        for i, (src, dst) in enumerate(((pos_hbm, pos), (tb_hbm, tb), (sb_hbm, sb), (th_hbm, th), (sh_hbm, sh)))
    ]
    barrier = pltpu.get_barrier_semaphore()
    clerk = tok == CLERK
    for k, r in ((2, 0), (2, 1), (1, 0), (1, 1), (3, 0), (3, 1), (0, 1)):
        @pl.when(device(k, r)[0] != CLERK)
        def _():
            pl.semaphore_signal(barrier, inc=1, device_id=device(k, r), device_id_type=MESH)

    for load in loads:
        load.start()

    loads[0].wait()
    sub = lax.broadcasted_iota(jnp.int32, (TOK, TOK), 0)
    lane = lax.broadcasted_iota(jnp.int32, (TOK, TOK), 1)
    spread = jnp.where(sub == lane, jnp.broadcast_to(pos[...], (TOK, TOK)), 0).astype(F32)
    column = jnp.sum(spread, axis=1, keepdims=True).astype(jnp.int32)
    onehot = (lax.broadcasted_iota(jnp.int32, (TOK, tb.shape[0]), 1) == column).astype(BF16)
    loads[1].wait()
    loads[2].wait()

    def pick(k):
        yk = (y + k) % NY
        t_off = pl.multiple_of(yk * (NC * width_t), 128)
        s_off = pl.multiple_of(yk * (NC * width_s), 128)
        t_rows = jnp.dot(onehot, tb[:, pl.ds(t_off, NC * width_t)], preferred_element_type=F32)
        s_rows = jnp.dot(onehot, sb[:, pl.ds(s_off, NC * width_s)], preferred_element_type=F32)
        for h in range(NC):
            picked[k, h, :, :width_t] = t_rows[:, h * width_t : (h + 1) * width_t].astype(BF16)
            picked[k, h, :, width_t : width_t + width_s] = s_rows[:, h * width_s : (h + 1) * width_s].astype(BF16)

    pick(2)

    @pl.when(jnp.logical_not(clerk))
    def _():
        pl.semaphore_wait(barrier, NY * NC - 1)

    @pl.when(device(0, 1)[0] == CLERK)
    def _():
        pl.semaphore_signal(go, inc=1, device_id=device(0, 1), device_id_type=MESH)

    @pl.when(clerk)
    def _():
        pl.semaphore_wait(go, 1)

    sent = []
    arrived = {}

    def start(copy):
        copy.start()
        sent.append(copy)
        return copy

    for k in (2, 1, 3, 0):
        if k != 2:
            pick(k)
        for r in range(NC):
            if (k, r) != (0, 0):
                slot = slot_of(BACK[k], r)
                arrived[BACK[k], r] = start(remote(
                    picked.at[k, (c + r) % NC],
                    states.at[slot * TOK : (slot + 1) * TOK],
                    st_send.at[slot], st_recv.at[slot], device(k, r),
                ))
    states[:TOK] = picked[0, c]

    for dx, dz in [(0, dz) for dz in range(1, NZ)] + [(dx, 0) for dx in range(1, NX)]:
        there = (CLERK, device(0, 0, dx, dz)[1])
        pl.semaphore_signal(barrier, inc=1, device_id=there, device_id_type=MESH)

    def multiply(ks):
        first = min(PLACE[k] for k in ks) * PAIR
        rows = slice(first, first + len(ks) * PAIR)
        for m in range(2):
            if m == 0:
                part[m, rows] = jnp.dot(states[rows, :width_t], th[...], preferred_element_type=F32)
            else:
                part[m, rows] = jnp.dot(
                    states[rows, width_t : width_t + width_s], sh[...], preferred_element_type=F32
                )
            for k in ks:
                at = PLACE[k]
                sib_copies[m, k] = start(remote(
                    part.at[m, at * PAIR + TOK : (at + 1) * PAIR],
                    sib.at[m, at], sib_send.at[m, at], sib_recv.at[m, at], device(0, 1),
                ))

    def add_cores(m, k):
        sib_copies[m, k].wait_recv()
        at = PLACE[k]
        chip[m, at] = part[m, at * PAIR : at * PAIR + TOK] + sib[m, at]

    sib_copies = {}
    loads[3].wait()
    loads[4].wait()
    arrived[0, 1].wait_recv()
    multiply((0,))
    for r in range(NC):
        arrived[2, r].wait_recv()
    multiply((2,))

    opp_copies = []
    for m, k in ((0, 1), (1, 3)):
        add_cores(m, 2)
        opp_copies.append(start(remote(
            chip.at[m, PLACE[2]], opp.at[m], opp_send.at[m], opp_recv.at[m], device(k, 0)
        )))
    for k in (1, 3):
        for r in range(NC):
            arrived[k, r].wait_recv()
    multiply((1, 3))
    ring_copies = {}
    for m, k in ((1, 1), (0, 3)):
        add_cores(m, k)
        ring_copies[m, k] = start(remote(
            chip.at[m, PLACE[k]], ring.at[m, k // 2], ring_send.at[m, k // 2], ring_recv.at[m, k // 2], device(k, 0)
        ))
    for m, k in ((0, 1), (1, 3)):
        add_cores(m, k)
    for m, k in ((0, 1), (1, 3)):
        opp_copies[m].wait_recv()
        merged[m] = chip[m, PLACE[k]] + opp[m]
        ring_copies[m, k] = start(remote(
            merged.at[m], ring.at[m, k // 2], ring_send.at[m, k // 2], ring_recv.at[m, k // 2], device(k, 0)
        ))
    @pl.when(clerk)
    def _():
        pl.semaphore_wait(barrier, NY * NC * (NZ - 1 + NX - 1))
        for k, r in ((2, 0), (2, 1), (1, 0), (1, 1), (3, 0), (3, 1), (0, 1)):
            pl.semaphore_signal(far, inc=1, device_id=device(k, r), device_id_type=MESH)

    add_cores(0, 0)
    add_cores(1, 0)
    cols_ref[...] = jnp.transpose(states[:, width_t : width_t + width_s].astype(F32)).astype(BF16)

    for copy in ring_copies.values():
        copy.wait_recv()
    t_log = chip[0, 0] + (ring[0, 0] + ring[0, 1])
    s_log = chip[1, 0] + (ring[1, 0] + ring[1, 1])
    logits[0, 0] = t_log
    logits[0, 1] = s_log

    top_t = jnp.max(t_log, axis=1, keepdims=True)
    top_s = jnp.max(s_log, axis=1, keepdims=True)
    exp_t = jnp.exp(t_log - top_t)
    exp_s = jnp.exp(s_log - top_s)
    columns = [
        jnp.sum(exp_t, axis=1, keepdims=True),
        jnp.sum(exp_t * t_log, axis=1, keepdims=True),
        jnp.sum(exp_t * s_log, axis=1, keepdims=True),
        jnp.sum(exp_s, axis=1, keepdims=True),
        top_t, top_t, top_t, top_s,
    ]
    sub = lax.broadcasted_iota(jnp.int32, (TOK, 128), 0)
    lane = lax.broadcasted_iota(jnp.int32, (TOK, 128), 1)
    packed = jnp.zeros((TOK, 128), F32)
    for k, value in enumerate(columns):
        packed = jnp.where(lane == sub + k * TOK, value, packed)
    zbuf[0:1] = jnp.sum(packed, axis=0, keepdims=True)

    @pl.when(jnp.logical_not(clerk))
    def _():
        pl.semaphore_wait(far, 1)

    for dz in sorted(range(1, NZ), key=lambda d: -min(d, NZ - d)):
        remote(zbuf.at[0:1], zbuf.at[NZ - dz : NZ - dz + 1], z_sem.at[0], z_sem.at[1], device(0, 0, 0, dz)).start()

    def pass_logits(m, source, slot, target):
        start(remote(logits.at[source, m], logits.at[slot, m], lg_send.at[slot, m], lg_recv.at[slot, m], target))

    def arrive(m, k, r):
        slot = slot_of(k, r)
        landed = logits.at[slot, m]
        pltpu.make_async_copy(landed, landed, lg_recv.at[slot, m]).wait()
        if r == 0:
            if (m, k) == (0, 3):
                pass_logits(m, slot, slot_of(2, 0), device(1, 0))
            if (m, k) == (1, 1):
                pass_logits(m, slot, slot_of(2, 0), device(3, 0))
            pass_logits(m, slot, slot_of(k, 1), device(0, 1))

    def exponents(m, k, r):
        slot = slot_of(k, r)
        values = logits[slot, m]
        top = jnp.max(values, axis=1, keepdims=True)
        shifted[slot, m] = jnp.exp(values - top)
        tops[slot, m] = jnp.broadcast_to(top, (TOK, 128))

    for m, k in ((0, 1), (1, 3), (1, 1), (0, 3)):
        pass_logits(m, 0, slot_of(BACK[k], 0), device(k, 0))
    for m in range(2):
        pass_logits(m, 0, slot_of(0, 1), device(0, 1))

    shifted[0, 0] = exp_t
    shifted[0, 1] = exp_s
    tops[0, 0] = jnp.broadcast_to(top_t, (TOK, 128))
    tops[0, 1] = jnp.broadcast_to(top_s, (TOK, 128))
    for m in range(2):
        arrive(m, 0, 1)
        exponents(m, 0, 1)
    for m, k in ((0, 3), (1, 1), (1, 3), (0, 1)):
        arrive(m, k, 0)
    for m, k in ((0, 3), (1, 1), (1, 3), (0, 1)):
        exponents(m, k, 0)

    pltpu.make_async_copy(zbuf.at[1:NZ], zbuf.at[1:NZ], z_sem.at[1]).wait()
    pbuf[0:1] = combine(zbuf[...].reshape(NZ, 1, 128))
    plane = [(dx, k, r) for dx in (2, 1, 3, 0) for k in (2, 1, 3, 0) for r in range(NC) if (dx, k, r) != (0, 0, 0)]
    for dx, k, r in plane:
        row = BACK[dx] * NY * NC + slot_of(BACK[k], r)
        remote(pbuf.at[0:1], pbuf.at[row : row + 1], p_sem.at[0], p_sem.at[1], device(k, r, dx)).start()

    for m in range(2):
        arrive(m, 2, 0)
    for m, k in ((0, 3), (1, 1), (1, 3), (0, 1)):
        arrive(m, k, 1)
        exponents(m, k, 1)
    for m in range(2):
        exponents(m, 2, 0)
    for m in range(2):
        arrive(m, 2, 1)
        exponents(m, 2, 1)

    for copy in sent:
        copy.wait_send()
    everyone = pbuf.at[1 : NX * NY * NC]
    pltpu.make_async_copy(zbuf.at[1:NZ], zbuf.at[1:NZ], z_sem.at[0]).wait()
    pltpu.make_async_copy(everyone, everyone, p_sem.at[0]).wait()
    pltpu.make_async_copy(everyone, everyone, p_sem.at[1]).wait()
    rows = combine(pbuf[...].reshape(NX, NY * NC, 128))

    sum_t = rows
    t_lse = lanes(rows, 4 * TOK) + jnp.log(sum_t)
    s_lse = lanes(rows, 7 * TOK) + jnp.log(lanes(rows, 3 * TOK))
    entropy = t_lse - lanes(rows, TOK) / sum_t
    log_weight = entropy * (-2.0 / math.log(vocab))
    loss_ref[...] = (jnp.exp(log_weight) * (s_lse - lanes(rows, 2 * TOK) / sum_t - entropy))[0:1]
    log_scale = log_weight + math.log(vocab / TOK)

    lane = lax.broadcasted_iota(jnp.int32, (NY * NC, TOK, 128), 2)
    sub = lax.broadcasted_iota(jnp.int32, (NY * NC, TOK, 128), 1)

    def column_of(values):
        spread = jnp.broadcast_to(values[:, None, :], (NY * NC, TOK, 128))
        return jnp.sum(jnp.where(lane == sub, spread, 0.0), axis=2, keepdims=True)

    scale_t = jnp.exp(tops[:, 0] + column_of(log_scale - t_lse))
    scale_s = jnp.exp(tops[:, 1] + column_of(log_scale - s_lse))
    for slot in range(NY * NC):
        for at in range(0, shard, 128):
            cut = slice(at, at + 128)
            grad = scale_s[slot] * shifted[slot, 1, :, cut] - scale_t[slot] * shifted[slot, 0, :, cut]
            grad_ref[slot * TOK : (slot + 1) * TOK, cut] = grad.astype(BF16)


def final_kernel(pieces, cols_ref, grad_ref, loss_in, head_hbm, loss_hbm, head, loss, sem):
    loss[...] = loss_in[:, :TOK]
    copies = [pltpu.make_async_copy(loss, loss_hbm, sem.at[pieces])]
    copies[0].start()
    tall = head.shape[0] // pieces
    for i in range(pieces):
        at = slice(i * tall, (i + 1) * tall)
        head[at] = jnp.dot(cols_ref[at], grad_ref[...], preferred_element_type=F32).astype(BF16)
        copies.append(pltpu.make_async_copy(head.at[at], head_hbm.at[at], sem.at[i]))
        copies[-1].start()
    for copy in copies:
        copy.wait()


def on_device(teacher_batch, student_batch, positions, teacher_head, student_head):
    width_t, shard = teacher_head.shape
    width_s = student_head.shape[0]
    vocab = shard * NX * NZ
    wide = 128 * pl.cdiv(width_t + width_s, 128)
    groups = NY * NC
    hbm = pl.BlockSpec(memory_space=pltpu.HBM)
    in_hbm = functools.partial(pltpu.with_memory_space_constraint, memory_space=pltpu.HBM)
    vmem = pl.BlockSpec(memory_space=pltpu.VMEM)
    dma = pltpu.SemaphoreType.DMA
    grad, cols, loss = pl.pallas_call(
        functools.partial(exchange_kernel, vocab, width_t, width_s, shard),
        out_shape=(
            pltpu.VMEM((ROWS, shard), BF16),
            pltpu.VMEM((width_s, ROWS), BF16),
            pltpu.VMEM((1, 128), F32),
        ),
        in_specs=[hbm] * 5,
        out_specs=(vmem, vmem, vmem),
        scratch_shapes=[
            pltpu.VMEM(teacher_batch.shape, BF16),
            pltpu.VMEM(student_batch.shape, BF16),
            pltpu.VMEM((1, TOK), jnp.int32),
            pltpu.VMEM(teacher_head.shape, BF16),
            pltpu.VMEM(student_head.shape, BF16),
            pltpu.VMEM((NY, NC, TOK, wide), BF16),
            pltpu.VMEM((ROWS, wide), BF16),
            pltpu.VMEM((2, ROWS, shard), F32),
            pltpu.VMEM((2, NY, TOK, shard), F32),
            pltpu.VMEM((2, NY, TOK, shard), F32),
            pltpu.VMEM((2, TOK, shard), F32),
            pltpu.VMEM((2, TOK, shard), F32),
            pltpu.VMEM((2, 2, TOK, shard), F32),
            pltpu.VMEM((groups, 2, TOK, shard), F32),
            pltpu.VMEM((groups, 2, TOK, shard), F32),
            pltpu.VMEM((groups, 2, TOK, 128), F32),
            pltpu.VMEM((NZ, 128), F32),
            pltpu.VMEM((NX * groups, 128), F32),
            dma((5,)),
            dma((groups,)), dma((groups,)),
            dma((2, NY)), dma((2, NY)),
            dma((2,)), dma((2,)),
            dma((2, 2)), dma((2, 2)),
            dma((groups, 2)), dma((groups, 2)),
            dma((2,)), dma((2,)),
            pltpu.SemaphoreType.REGULAR,
            pltpu.SemaphoreType.REGULAR,
        ],
        compiler_params=pltpu.CompilerParams(
            collective_id=0, has_side_effects=True, vmem_limit_bytes=32 * 1024 * 1024
        ),
    )(*map(in_hbm, (teacher_batch, student_batch, positions.reshape(1, TOK), teacher_head, student_head)))
    pieces = 4
    head_grad, loss = pl.pallas_call(
        functools.partial(final_kernel, pieces),
        out_shape=(
            jax.ShapeDtypeStruct((width_s, shard), BF16),
            jax.ShapeDtypeStruct((1, TOK), F32),
        ),
        in_specs=[vmem] * 3,
        out_specs=(hbm, hbm),
        scratch_shapes=[pltpu.VMEM((width_s, shard), BF16), pltpu.VMEM((1, TOK), F32), dma((pieces + 1,))],
        compiler_params=pltpu.CompilerParams(vmem_limit_bytes=16 * 1024 * 1024),
    )(cols, grad, loss)
    return head_grad, loss.reshape(TOK)


def solution(mesh):
    in_specs = (P("tok", None), P("tok", None), P("tok"), P("tok", "voc"), P("tok", "voc"))
    out_specs = (P("tok", "voc"), P("tok"))
    return jax.shard_map(
        on_device, mesh=mesh, in_specs=in_specs, out_specs=out_specs, check_vma=False
    )
```

```python
import functools
import math

import jax
import jax.numpy as jnp
from jax import lax
from jax.experimental import pallas as pl
from jax.experimental.pallas import tpu as pltpu
from jax.sharding import PartitionSpec as P

MESH = pl.DeviceIdType.MESH
F32 = jnp.float32
BF16 = jnp.bfloat16
NY, NC, NX, NZ = 4, 2, 4, 16
TOK = 16
CLERK = 4
PAIR = NC * TOK
ROWS = NY * PAIR
PLACE = {0: 0, 1: 1, 3: 2, 2: 3}
BACK = {0: 0, 1: 3, 2: 2, 3: 1}


def slot_of(k, r):
    return PLACE[k] * NC + r


def remote(src, dst, send, recv, target):
    return pltpu.make_async_remote_copy(
        src_ref=src, dst_ref=dst, send_sem=send, recv_sem=recv, device_id=target, device_id_type=MESH
    )


def lanes(values, start):
    return pltpu.roll(values, (128 - start) % 128, axis=values.ndim - 1) if start else values


def combine(rows):
    tops = pltpu.roll(rows, 64, axis=2)
    top = jnp.max(tops, axis=0)
    total = jnp.sum(rows * jnp.exp(tops - top[None]), axis=0)
    lane = lax.broadcasted_iota(jnp.int32, total.shape, 1)
    return jnp.where(lane < 64, total, pltpu.roll(top, 64, axis=1))


def exchange_kernel(
    vocab, width_t, width_s, shard,
    tb_hbm, sb_hbm, pos_hbm, th_hbm, sh_hbm,
    grad_ref, cols_ref, loss_ref,
    tb, sb, pos, th, sh, picked, states, part, sib, chip, opp, merged, ring, logits, shifted, tops, zbuf, pbuf,
    load_sem, st_send, st_recv, sib_send, sib_recv, opp_send, opp_recv, ring_send, ring_recv,
    lg_send, lg_recv, z_sem, p_sem, go, far,
):
    tok, voc = lax.axis_index("tok"), lax.axis_index("voc")
    y, c = tok // NC, tok % NC
    z, x = voc // NX, voc % NX

    def device(k, r, dx=0, dz=0):
        return (((y + k) % NY) * NC + (c + r) % NC, ((z + dz) % NZ) * NX + (x + dx) % NX)

    loads = [
        pltpu.make_async_copy(src, dst, load_sem.at[i])
        for i, (src, dst) in enumerate(((pos_hbm, pos), (tb_hbm, tb), (sb_hbm, sb), (th_hbm, th), (sh_hbm, sh)))
    ]
    barrier = pltpu.get_barrier_semaphore()
    clerk = tok == CLERK
    for k, r in ((2, 0), (2, 1), (1, 0), (1, 1), (3, 0), (3, 1), (0, 1)):
        @pl.when(device(k, r)[0] != CLERK)
        def _():
            pl.semaphore_signal(barrier, inc=1, device_id=device(k, r), device_id_type=MESH)

    for load in loads:
        load.start()

    loads[0].wait()
    sub = lax.broadcasted_iota(jnp.int32, (TOK, TOK), 0)
    lane = lax.broadcasted_iota(jnp.int32, (TOK, TOK), 1)
    spread = jnp.where(sub == lane, jnp.broadcast_to(pos[...], (TOK, TOK)), 0).astype(F32)
    column = jnp.sum(spread, axis=1, keepdims=True).astype(jnp.int32)
    onehot = (lax.broadcasted_iota(jnp.int32, (TOK, tb.shape[0]), 1) == column).astype(BF16)
    loads[1].wait()
    loads[2].wait()

    def pick(k):
        yk = (y + k) % NY
        t_off = pl.multiple_of(yk * (NC * width_t), 128)
        s_off = pl.multiple_of(yk * (NC * width_s), 128)
        t_rows = jnp.dot(onehot, tb[:, pl.ds(t_off, NC * width_t)], preferred_element_type=F32)
        s_rows = jnp.dot(onehot, sb[:, pl.ds(s_off, NC * width_s)], preferred_element_type=F32)
        for h in range(NC):
            picked[k, h, :, :width_t] = t_rows[:, h * width_t : (h + 1) * width_t].astype(BF16)
            picked[k, h, :, width_t : width_t + width_s] = s_rows[:, h * width_s : (h + 1) * width_s].astype(BF16)

    pick(2)

    @pl.when(jnp.logical_not(clerk))
    def _():
        pl.semaphore_wait(barrier, NY * NC - 1)

    @pl.when(device(0, 1)[0] == CLERK)
    def _():
        pl.semaphore_signal(go, inc=1, device_id=device(0, 1), device_id_type=MESH)

    @pl.when(clerk)
    def _():
        pl.semaphore_wait(go, 1)

    sent = []
    arrived = {}

    def start(copy):
        copy.start()
        sent.append(copy)
        return copy

    for k in (2, 1, 3, 0):
        if k != 2:
            pick(k)
        for r in range(NC):
            if (k, r) != (0, 0):
                slot = slot_of(BACK[k], r)
                arrived[BACK[k], r] = start(remote(
                    picked.at[k, (c + r) % NC],
                    states.at[slot * TOK : (slot + 1) * TOK],
                    st_send.at[slot], st_recv.at[slot], device(k, r),
                ))
    states[:TOK] = picked[0, c]

    for dx, dz in [(0, dz) for dz in range(1, NZ)] + [(dx, 0) for dx in range(1, NX)]:
        there = (CLERK, device(0, 0, dx, dz)[1])
        pl.semaphore_signal(barrier, inc=1, device_id=there, device_id_type=MESH)

    def multiply(ks):
        first = min(PLACE[k] for k in ks) * PAIR
        rows = slice(first, first + len(ks) * PAIR)
        for m in range(2):
            if m == 0:
                part[m, rows] = jnp.dot(states[rows, :width_t], th[...], preferred_element_type=F32)
            else:
                part[m, rows] = jnp.dot(
                    states[rows, width_t : width_t + width_s], sh[...], preferred_element_type=F32
                )
            for k in ks:
                at = PLACE[k]
                sib_copies[m, k] = start(remote(
                    part.at[m, at * PAIR + TOK : (at + 1) * PAIR],
                    sib.at[m, at], sib_send.at[m, at], sib_recv.at[m, at], device(0, 1),
                ))

    def add_cores(m, k):
        sib_copies[m, k].wait_recv()
        at = PLACE[k]
        chip[m, at] = part[m, at * PAIR : at * PAIR + TOK] + sib[m, at]

    sib_copies = {}
    loads[3].wait()
    loads[4].wait()
    arrived[0, 1].wait_recv()
    multiply((0,))
    for r in range(NC):
        arrived[2, r].wait_recv()
    multiply((2,))

    opp_copies = []
    for m, k in ((0, 1), (1, 3)):
        add_cores(m, 2)
        opp_copies.append(start(remote(
            chip.at[m, PLACE[2]], opp.at[m], opp_send.at[m], opp_recv.at[m], device(k, 0)
        )))
    for k in (1, 3):
        for r in range(NC):
            arrived[k, r].wait_recv()
    multiply((1, 3))
    ring_copies = {}
    for m, k in ((1, 1), (0, 3)):
        add_cores(m, k)
        ring_copies[m, k] = start(remote(
            chip.at[m, PLACE[k]], ring.at[m, k // 2], ring_send.at[m, k // 2], ring_recv.at[m, k // 2], device(k, 0)
        ))
    for m, k in ((0, 1), (1, 3)):
        add_cores(m, k)
    @pl.when(clerk)
    def _():
        pl.semaphore_wait(barrier, NY * NC * (NZ - 1 + NX - 1))
        for k, r in ((2, 0), (2, 1), (1, 0), (1, 1), (3, 0), (3, 1), (0, 1)):
            pl.semaphore_signal(far, inc=1, device_id=device(k, r), device_id_type=MESH)

    for m, k in ((0, 1), (1, 3)):
        opp_copies[m].wait_recv()
        merged[m] = chip[m, PLACE[k]] + opp[m]
        ring_copies[m, k] = start(remote(
            merged.at[m], ring.at[m, k // 2], ring_send.at[m, k // 2], ring_recv.at[m, k // 2], device(k, 0)
        ))
    add_cores(0, 0)
    add_cores(1, 0)
    cols_ref[...] = jnp.transpose(states[:, width_t : width_t + width_s].astype(F32)).astype(BF16)

    for copy in ring_copies.values():
        copy.wait_recv()
    t_log = chip[0, 0] + (ring[0, 0] + ring[0, 1])
    s_log = chip[1, 0] + (ring[1, 0] + ring[1, 1])
    logits[0, 0] = t_log
    logits[0, 1] = s_log

    top_t = jnp.max(t_log, axis=1, keepdims=True)
    top_s = jnp.max(s_log, axis=1, keepdims=True)
    exp_t = jnp.exp(t_log - top_t)
    exp_s = jnp.exp(s_log - top_s)
    columns = [
        jnp.sum(exp_t, axis=1, keepdims=True),
        jnp.sum(exp_t * t_log, axis=1, keepdims=True),
        jnp.sum(exp_t * s_log, axis=1, keepdims=True),
        jnp.sum(exp_s, axis=1, keepdims=True),
        top_t, top_t, top_t, top_s,
    ]
    sub = lax.broadcasted_iota(jnp.int32, (TOK, 128), 0)
    lane = lax.broadcasted_iota(jnp.int32, (TOK, 128), 1)
    packed = jnp.zeros((TOK, 128), F32)
    for k, value in enumerate(columns):
        packed = jnp.where(lane == sub + k * TOK, value, packed)
    zbuf[0:1] = jnp.sum(packed, axis=0, keepdims=True)

    @pl.when(jnp.logical_not(clerk))
    def _():
        pl.semaphore_wait(far, 1)

    for dz in sorted(range(1, NZ), key=lambda d: -min(d, NZ - d)):
        remote(zbuf.at[0:1], zbuf.at[NZ - dz : NZ - dz + 1], z_sem.at[0], z_sem.at[1], device(0, 0, 0, dz)).start()

    def pass_logits(m, source, slot, target):
        start(remote(logits.at[source, m], logits.at[slot, m], lg_send.at[slot, m], lg_recv.at[slot, m], target))

    def arrive(m, k, r):
        slot = slot_of(k, r)
        landed = logits.at[slot, m]
        pltpu.make_async_copy(landed, landed, lg_recv.at[slot, m]).wait()
        if r == 0:
            if (m, k) == (0, 3):
                pass_logits(m, slot, slot_of(2, 0), device(1, 0))
            if (m, k) == (1, 1):
                pass_logits(m, slot, slot_of(2, 0), device(3, 0))
            pass_logits(m, slot, slot_of(k, 1), device(0, 1))

    def exponents(m, k, r):
        slot = slot_of(k, r)
        values = logits[slot, m]
        top = jnp.max(values, axis=1, keepdims=True)
        shifted[slot, m] = jnp.exp(values - top)
        tops[slot, m] = jnp.broadcast_to(top, (TOK, 128))

    for m, k in ((0, 1), (1, 3), (1, 1), (0, 3)):
        pass_logits(m, 0, slot_of(BACK[k], 0), device(k, 0))
    for m in range(2):
        pass_logits(m, 0, slot_of(0, 1), device(0, 1))

    shifted[0, 0] = exp_t
    shifted[0, 1] = exp_s
    tops[0, 0] = jnp.broadcast_to(top_t, (TOK, 128))
    tops[0, 1] = jnp.broadcast_to(top_s, (TOK, 128))
    for m in range(2):
        arrive(m, 0, 1)
        exponents(m, 0, 1)
    for m, k in ((0, 3), (1, 1), (1, 3), (0, 1)):
        arrive(m, k, 0)
    for m, k in ((0, 3), (1, 1), (1, 3), (0, 1)):
        exponents(m, k, 0)

    pltpu.make_async_copy(zbuf.at[1:NZ], zbuf.at[1:NZ], z_sem.at[1]).wait()
    pbuf[0:1] = combine(zbuf[...].reshape(NZ, 1, 128))
    plane = [(dx, k, r) for dx in (2, 1, 3, 0) for k in (2, 1, 3, 0) for r in range(NC) if (dx, k, r) != (0, 0, 0)]
    for dx, k, r in plane:
        row = BACK[dx] * NY * NC + slot_of(BACK[k], r)
        remote(pbuf.at[0:1], pbuf.at[row : row + 1], p_sem.at[0], p_sem.at[1], device(k, r, dx)).start()

    for m in range(2):
        arrive(m, 2, 0)
    for m, k in ((0, 3), (1, 1), (1, 3), (0, 1)):
        arrive(m, k, 1)
        exponents(m, k, 1)
    for m in range(2):
        exponents(m, 2, 0)
    for m in range(2):
        arrive(m, 2, 1)
        exponents(m, 2, 1)

    for copy in sent:
        copy.wait_send()
    everyone = pbuf.at[1 : NX * NY * NC]
    pltpu.make_async_copy(zbuf.at[1:NZ], zbuf.at[1:NZ], z_sem.at[0]).wait()
    pltpu.make_async_copy(everyone, everyone, p_sem.at[0]).wait()
    pltpu.make_async_copy(everyone, everyone, p_sem.at[1]).wait()
    rows = combine(pbuf[...].reshape(NX, NY * NC, 128))

    sum_t = rows
    t_lse = lanes(rows, 4 * TOK) + jnp.log(sum_t)
    s_lse = lanes(rows, 7 * TOK) + jnp.log(lanes(rows, 3 * TOK))
    entropy = t_lse - lanes(rows, TOK) / sum_t
    log_weight = entropy * (-2.0 / math.log(vocab))
    loss_ref[...] = (jnp.exp(log_weight) * (s_lse - lanes(rows, 2 * TOK) / sum_t - entropy))[0:1]
    log_scale = log_weight + math.log(vocab / TOK)

    lane = lax.broadcasted_iota(jnp.int32, (NY * NC, TOK, 128), 2)
    sub = lax.broadcasted_iota(jnp.int32, (NY * NC, TOK, 128), 1)

    def column_of(values):
        spread = jnp.broadcast_to(values[:, None, :], (NY * NC, TOK, 128))
        return jnp.sum(jnp.where(lane == sub, spread, 0.0), axis=2, keepdims=True)

    scale_t = jnp.exp(tops[:, 0] + column_of(log_scale - t_lse))
    scale_s = jnp.exp(tops[:, 1] + column_of(log_scale - s_lse))
    for slot in range(NY * NC):
        for at in range(0, shard, 128):
            cut = slice(at, at + 128)
            grad = scale_s[slot] * shifted[slot, 1, :, cut] - scale_t[slot] * shifted[slot, 0, :, cut]
            grad_ref[slot * TOK : (slot + 1) * TOK, cut] = grad.astype(BF16)


def final_kernel(pieces, cols_ref, grad_ref, loss_in, head_hbm, loss_hbm, head, loss, sem):
    loss[...] = loss_in[:, :TOK]
    copies = [pltpu.make_async_copy(loss, loss_hbm, sem.at[pieces])]
    copies[0].start()
    tall = head.shape[0] // pieces
    for i in range(pieces):
        at = slice(i * tall, (i + 1) * tall)
        head[at] = jnp.dot(cols_ref[at], grad_ref[...], preferred_element_type=F32).astype(BF16)
        copies.append(pltpu.make_async_copy(head.at[at], head_hbm.at[at], sem.at[i]))
        copies[-1].start()
    for copy in copies:
        copy.wait()


def on_device(teacher_batch, student_batch, positions, teacher_head, student_head):
    width_t, shard = teacher_head.shape
    width_s = student_head.shape[0]
    vocab = shard * NX * NZ
    wide = 128 * pl.cdiv(width_t + width_s, 128)
    groups = NY * NC
    hbm = pl.BlockSpec(memory_space=pltpu.HBM)
    in_hbm = functools.partial(pltpu.with_memory_space_constraint, memory_space=pltpu.HBM)
    vmem = pl.BlockSpec(memory_space=pltpu.VMEM)
    dma = pltpu.SemaphoreType.DMA
    grad, cols, loss = pl.pallas_call(
        functools.partial(exchange_kernel, vocab, width_t, width_s, shard),
        out_shape=(
            pltpu.VMEM((ROWS, shard), BF16),
            pltpu.VMEM((width_s, ROWS), BF16),
            pltpu.VMEM((1, 128), F32),
        ),
        in_specs=[hbm] * 5,
        out_specs=(vmem, vmem, vmem),
        scratch_shapes=[
            pltpu.VMEM(teacher_batch.shape, BF16),
            pltpu.VMEM(student_batch.shape, BF16),
            pltpu.VMEM((1, TOK), jnp.int32),
            pltpu.VMEM(teacher_head.shape, BF16),
            pltpu.VMEM(student_head.shape, BF16),
            pltpu.VMEM((NY, NC, TOK, wide), BF16),
            pltpu.VMEM((ROWS, wide), BF16),
            pltpu.VMEM((2, ROWS, shard), F32),
            pltpu.VMEM((2, NY, TOK, shard), F32),
            pltpu.VMEM((2, NY, TOK, shard), F32),
            pltpu.VMEM((2, TOK, shard), F32),
            pltpu.VMEM((2, TOK, shard), F32),
            pltpu.VMEM((2, 2, TOK, shard), F32),
            pltpu.VMEM((groups, 2, TOK, shard), F32),
            pltpu.VMEM((groups, 2, TOK, shard), F32),
            pltpu.VMEM((groups, 2, TOK, 128), F32),
            pltpu.VMEM((NZ, 128), F32),
            pltpu.VMEM((NX * groups, 128), F32),
            dma((5,)),
            dma((groups,)), dma((groups,)),
            dma((2, NY)), dma((2, NY)),
            dma((2,)), dma((2,)),
            dma((2, 2)), dma((2, 2)),
            dma((groups, 2)), dma((groups, 2)),
            dma((2,)), dma((2,)),
            pltpu.SemaphoreType.REGULAR,
            pltpu.SemaphoreType.REGULAR,
        ],
        compiler_params=pltpu.CompilerParams(
            collective_id=0, has_side_effects=True, vmem_limit_bytes=32 * 1024 * 1024
        ),
    )(*map(in_hbm, (teacher_batch, student_batch, positions.reshape(1, TOK), teacher_head, student_head)))
    pieces = 4
    head_grad, loss = pl.pallas_call(
        functools.partial(final_kernel, pieces),
        out_shape=(
            jax.ShapeDtypeStruct((width_s, shard), BF16),
            jax.ShapeDtypeStruct((1, TOK), F32),
        ),
        in_specs=[vmem] * 3,
        out_specs=(hbm, hbm),
        scratch_shapes=[pltpu.VMEM((width_s, shard), BF16), pltpu.VMEM((1, TOK), F32), dma((pieces + 1,))],
        compiler_params=pltpu.CompilerParams(vmem_limit_bytes=16 * 1024 * 1024),
    )(cols, grad, loss)
    return head_grad, loss.reshape(TOK)


def solution(mesh):
    in_specs = (P("tok", None), P("tok", None), P("tok"), P("tok", "voc"), P("tok", "voc"))
    out_specs = (P("tok", "voc"), P("tok"))
    return jax.shard_map(
        on_device, mesh=mesh, in_specs=in_specs, out_specs=out_specs, check_vma=False
    )
```

```python
import functools
import math

import jax
import jax.numpy as jnp
from jax import lax
from jax.experimental import pallas as pl
from jax.experimental.pallas import tpu as pltpu
from jax.sharding import PartitionSpec as P

MESH = pl.DeviceIdType.MESH
F32 = jnp.float32
BF16 = jnp.bfloat16
NY, NC, NX, NZ = 4, 2, 4, 16
TOK = 16
CLERK = 4
PAIR = NC * TOK
ROWS = NY * PAIR
PLACE = {0: 0, 1: 1, 3: 2, 2: 3}
BACK = {0: 0, 1: 3, 2: 2, 3: 1}


FAR_FIRST = sorted(
    [(0, dz) for dz in range(1, NZ)] + [(dx, 0) for dx in range(1, NX)],
    key=lambda step: -min(step[0], NX - step[0]) - min(step[1], NZ - step[1]),
)


def slot_of(k, r):
    return PLACE[k] * NC + r


def remote(src, dst, send, recv, target):
    return pltpu.make_async_remote_copy(
        src_ref=src, dst_ref=dst, send_sem=send, recv_sem=recv, device_id=target, device_id_type=MESH
    )


def lanes(values, start):
    return pltpu.roll(values, (128 - start) % 128, axis=values.ndim - 1) if start else values


def combine(rows):
    tops = pltpu.roll(rows, 64, axis=2)
    top = jnp.max(tops, axis=0)
    total = jnp.sum(rows * jnp.exp(tops - top[None]), axis=0)
    lane = lax.broadcasted_iota(jnp.int32, total.shape, 1)
    return jnp.where(lane < 64, total, pltpu.roll(top, 64, axis=1))


def exchange_kernel(
    vocab, width_t, width_s, shard,
    tb_hbm, sb_hbm, pos_hbm, th_hbm, sh_hbm,
    grad_ref, cols_ref, loss_ref,
    tb, sb, pos, th, sh, picked, states, part, sib, chip, opp, merged, ring, logits, shifted, tops, zbuf, pbuf,
    load_sem, st_send, st_recv, sib_send, sib_recv, opp_send, opp_recv, ring_send, ring_recv,
    lg_send, lg_recv, z_sem, p_sem, go, far,
):
    tok, voc = lax.axis_index("tok"), lax.axis_index("voc")
    y, c = tok // NC, tok % NC
    z, x = voc // NX, voc % NX

    def device(k, r, dx=0, dz=0):
        return (((y + k) % NY) * NC + (c + r) % NC, ((z + dz) % NZ) * NX + (x + dx) % NX)

    loads = [
        pltpu.make_async_copy(src, dst, load_sem.at[i])
        for i, (src, dst) in enumerate(((pos_hbm, pos), (tb_hbm, tb), (sb_hbm, sb), (th_hbm, th), (sh_hbm, sh)))
    ]
    barrier = pltpu.get_barrier_semaphore()
    clerk = tok == CLERK
    for k, r in ((2, 0), (2, 1), (1, 0), (1, 1), (3, 0), (3, 1), (0, 1)):
        @pl.when(device(k, r)[0] != CLERK)
        def _():
            pl.semaphore_signal(barrier, inc=1, device_id=device(k, r), device_id_type=MESH)

    for load in loads:
        load.start()

    loads[0].wait()
    sub = lax.broadcasted_iota(jnp.int32, (TOK, TOK), 0)
    lane = lax.broadcasted_iota(jnp.int32, (TOK, TOK), 1)
    spread = jnp.where(sub == lane, jnp.broadcast_to(pos[...], (TOK, TOK)), 0).astype(F32)
    column = jnp.sum(spread, axis=1, keepdims=True).astype(jnp.int32)
    onehot = (lax.broadcasted_iota(jnp.int32, (TOK, tb.shape[0]), 1) == column).astype(BF16)
    loads[1].wait()
    loads[2].wait()

    def pick(k):
        yk = (y + k) % NY
        t_off = pl.multiple_of(yk * (NC * width_t), 128)
        s_off = pl.multiple_of(yk * (NC * width_s), 128)
        t_rows = jnp.dot(onehot, tb[:, pl.ds(t_off, NC * width_t)], preferred_element_type=F32)
        s_rows = jnp.dot(onehot, sb[:, pl.ds(s_off, NC * width_s)], preferred_element_type=F32)
        for h in range(NC):
            picked[k, h, :, :width_t] = t_rows[:, h * width_t : (h + 1) * width_t].astype(BF16)
            picked[k, h, :, width_t : width_t + width_s] = s_rows[:, h * width_s : (h + 1) * width_s].astype(BF16)

    pick(2)

    @pl.when(jnp.logical_not(clerk))
    def _():
        pl.semaphore_wait(barrier, NY * NC - 1)

    @pl.when(device(0, 1)[0] == CLERK)
    def _():
        pl.semaphore_signal(go, inc=1, device_id=device(0, 1), device_id_type=MESH)

    @pl.when(clerk)
    def _():
        pl.semaphore_wait(go, 1)

    sent = []
    arrived = {}

    def start(copy):
        copy.start()
        sent.append(copy)
        return copy

    for k in (2, 1, 3, 0):
        if k != 2:
            pick(k)
        for r in range(NC):
            if (k, r) != (0, 0):
                slot = slot_of(BACK[k], r)
                arrived[BACK[k], r] = start(remote(
                    picked.at[k, (c + r) % NC],
                    states.at[slot * TOK : (slot + 1) * TOK],
                    st_send.at[slot], st_recv.at[slot], device(k, r),
                ))
    states[:TOK] = picked[0, c]

    for dx, dz in FAR_FIRST:
        there = (CLERK, device(0, 0, dx, dz)[1])
        pl.semaphore_signal(barrier, inc=1, device_id=there, device_id_type=MESH)

    def multiply(ks):
        first = min(PLACE[k] for k in ks) * PAIR
        rows = slice(first, first + len(ks) * PAIR)
        for m in range(2):
            if m == 0:
                part[m, rows] = jnp.dot(states[rows, :width_t], th[...], preferred_element_type=F32)
            else:
                part[m, rows] = jnp.dot(
                    states[rows, width_t : width_t + width_s], sh[...], preferred_element_type=F32
                )
            for k in ks:
                at = PLACE[k]
                sib_copies[m, k] = start(remote(
                    part.at[m, at * PAIR + TOK : (at + 1) * PAIR],
                    sib.at[m, at], sib_send.at[m, at], sib_recv.at[m, at], device(0, 1),
                ))

    def add_cores(m, k):
        sib_copies[m, k].wait_recv()
        at = PLACE[k]
        chip[m, at] = part[m, at * PAIR : at * PAIR + TOK] + sib[m, at]

    sib_copies = {}
    loads[3].wait()
    loads[4].wait()
    arrived[0, 1].wait_recv()
    multiply((0,))
    for r in range(NC):
        arrived[2, r].wait_recv()
    multiply((2,))

    opp_copies = []
    for m, k in ((0, 1), (1, 3)):
        add_cores(m, 2)
        opp_copies.append(start(remote(
            chip.at[m, PLACE[2]], opp.at[m], opp_send.at[m], opp_recv.at[m], device(k, 0)
        )))
    for k in (1, 3):
        for r in range(NC):
            arrived[k, r].wait_recv()
    multiply((1, 3))
    ring_copies = {}
    for m, k in ((1, 1), (0, 3)):
        add_cores(m, k)
        ring_copies[m, k] = start(remote(
            chip.at[m, PLACE[k]], ring.at[m, k // 2], ring_send.at[m, k // 2], ring_recv.at[m, k // 2], device(k, 0)
        ))
    for m, k in ((0, 1), (1, 3)):
        add_cores(m, k)
    @pl.when(clerk)
    def _():
        pl.semaphore_wait(barrier, NY * NC * (NZ - 1 + NX - 1))
        for k, r in ((2, 0), (2, 1), (1, 0), (1, 1), (3, 0), (3, 1), (0, 1)):
            pl.semaphore_signal(far, inc=1, device_id=device(k, r), device_id_type=MESH)

    for m, k in ((0, 1), (1, 3)):
        opp_copies[m].wait_recv()
        merged[m] = chip[m, PLACE[k]] + opp[m]
        ring_copies[m, k] = start(remote(
            merged.at[m], ring.at[m, k // 2], ring_send.at[m, k // 2], ring_recv.at[m, k // 2], device(k, 0)
        ))
    add_cores(0, 0)
    add_cores(1, 0)
    cols_ref[...] = jnp.transpose(states[:, width_t : width_t + width_s].astype(F32)).astype(BF16)

    for copy in ring_copies.values():
        copy.wait_recv()
    t_log = chip[0, 0] + (ring[0, 0] + ring[0, 1])
    s_log = chip[1, 0] + (ring[1, 0] + ring[1, 1])
    logits[0, 0] = t_log
    logits[0, 1] = s_log

    top_t = jnp.max(t_log, axis=1, keepdims=True)
    top_s = jnp.max(s_log, axis=1, keepdims=True)
    exp_t = jnp.exp(t_log - top_t)
    exp_s = jnp.exp(s_log - top_s)
    columns = [
        jnp.sum(exp_t, axis=1, keepdims=True),
        jnp.sum(exp_t * t_log, axis=1, keepdims=True),
        jnp.sum(exp_t * s_log, axis=1, keepdims=True),
        jnp.sum(exp_s, axis=1, keepdims=True),
        top_t, top_t, top_t, top_s,
    ]
    sub = lax.broadcasted_iota(jnp.int32, (TOK, 128), 0)
    lane = lax.broadcasted_iota(jnp.int32, (TOK, 128), 1)
    packed = jnp.zeros((TOK, 128), F32)
    for k, value in enumerate(columns):
        packed = jnp.where(lane == sub + k * TOK, value, packed)
    zbuf[0:1] = jnp.sum(packed, axis=0, keepdims=True)

    @pl.when(jnp.logical_not(clerk))
    def _():
        pl.semaphore_wait(far, 1)

    for dz in sorted(range(1, NZ), key=lambda d: -min(d, NZ - d)):
        remote(zbuf.at[0:1], zbuf.at[NZ - dz : NZ - dz + 1], z_sem.at[0], z_sem.at[1], device(0, 0, 0, dz)).start()

    def pass_logits(m, source, slot, target):
        start(remote(logits.at[source, m], logits.at[slot, m], lg_send.at[slot, m], lg_recv.at[slot, m], target))

    def arrive(m, k, r):
        slot = slot_of(k, r)
        landed = logits.at[slot, m]
        pltpu.make_async_copy(landed, landed, lg_recv.at[slot, m]).wait()
        if r == 0:
            if (m, k) == (0, 3):
                pass_logits(m, slot, slot_of(2, 0), device(1, 0))
            if (m, k) == (1, 1):
                pass_logits(m, slot, slot_of(2, 0), device(3, 0))
            pass_logits(m, slot, slot_of(k, 1), device(0, 1))

    def exponents(m, k, r):
        slot = slot_of(k, r)
        values = logits[slot, m]
        top = jnp.max(values, axis=1, keepdims=True)
        shifted[slot, m] = jnp.exp(values - top)
        tops[slot, m] = jnp.broadcast_to(top, (TOK, 128))

    for m, k in ((0, 1), (1, 3), (1, 1), (0, 3)):
        pass_logits(m, 0, slot_of(BACK[k], 0), device(k, 0))
    for m in range(2):
        pass_logits(m, 0, slot_of(0, 1), device(0, 1))

    shifted[0, 0] = exp_t
    shifted[0, 1] = exp_s
    tops[0, 0] = jnp.broadcast_to(top_t, (TOK, 128))
    tops[0, 1] = jnp.broadcast_to(top_s, (TOK, 128))
    for m in range(2):
        arrive(m, 0, 1)
        exponents(m, 0, 1)
    for m, k in ((0, 3), (1, 1), (1, 3), (0, 1)):
        arrive(m, k, 0)
    for m, k in ((0, 3), (1, 1), (1, 3), (0, 1)):
        exponents(m, k, 0)

    pltpu.make_async_copy(zbuf.at[1:NZ], zbuf.at[1:NZ], z_sem.at[1]).wait()
    pbuf[0:1] = combine(zbuf[...].reshape(NZ, 1, 128))
    plane = [(dx, k, r) for dx in (2, 1, 3, 0) for k in (2, 1, 3, 0) for r in range(NC) if (dx, k, r) != (0, 0, 0)]
    for dx, k, r in plane:
        row = BACK[dx] * NY * NC + slot_of(BACK[k], r)
        remote(pbuf.at[0:1], pbuf.at[row : row + 1], p_sem.at[0], p_sem.at[1], device(k, r, dx)).start()

    for m in range(2):
        arrive(m, 2, 0)
    for m, k in ((0, 3), (1, 1), (1, 3), (0, 1)):
        arrive(m, k, 1)
        exponents(m, k, 1)
    for m in range(2):
        exponents(m, 2, 0)
    for m in range(2):
        arrive(m, 2, 1)
        exponents(m, 2, 1)

    for copy in sent:
        copy.wait_send()
    everyone = pbuf.at[1 : NX * NY * NC]
    pltpu.make_async_copy(zbuf.at[1:NZ], zbuf.at[1:NZ], z_sem.at[0]).wait()
    pltpu.make_async_copy(everyone, everyone, p_sem.at[0]).wait()
    pltpu.make_async_copy(everyone, everyone, p_sem.at[1]).wait()
    rows = combine(pbuf[...].reshape(NX, NY * NC, 128))

    sum_t = rows
    t_lse = lanes(rows, 4 * TOK) + jnp.log(sum_t)
    s_lse = lanes(rows, 7 * TOK) + jnp.log(lanes(rows, 3 * TOK))
    entropy = t_lse - lanes(rows, TOK) / sum_t
    log_weight = entropy * (-2.0 / math.log(vocab))
    loss_ref[...] = (jnp.exp(log_weight) * (s_lse - lanes(rows, 2 * TOK) / sum_t - entropy))[0:1]
    log_scale = log_weight + math.log(vocab / TOK)

    lane = lax.broadcasted_iota(jnp.int32, (NY * NC, TOK, 128), 2)
    sub = lax.broadcasted_iota(jnp.int32, (NY * NC, TOK, 128), 1)

    def column_of(values):
        spread = jnp.broadcast_to(values[:, None, :], (NY * NC, TOK, 128))
        return jnp.sum(jnp.where(lane == sub, spread, 0.0), axis=2, keepdims=True)

    scale_t = jnp.exp(tops[:, 0] + column_of(log_scale - t_lse))
    scale_s = jnp.exp(tops[:, 1] + column_of(log_scale - s_lse))
    for slot in range(NY * NC):
        for at in range(0, shard, 128):
            cut = slice(at, at + 128)
            grad = scale_s[slot] * shifted[slot, 1, :, cut] - scale_t[slot] * shifted[slot, 0, :, cut]
            grad_ref[slot * TOK : (slot + 1) * TOK, cut] = grad.astype(BF16)


def final_kernel(pieces, cols_ref, grad_ref, loss_in, head_hbm, loss_hbm, head, loss, sem):
    loss[...] = loss_in[:, :TOK]
    copies = [pltpu.make_async_copy(loss, loss_hbm, sem.at[pieces])]
    copies[0].start()
    tall = head.shape[0] // pieces
    for i in range(pieces):
        at = slice(i * tall, (i + 1) * tall)
        head[at] = jnp.dot(cols_ref[at], grad_ref[...], preferred_element_type=F32).astype(BF16)
        copies.append(pltpu.make_async_copy(head.at[at], head_hbm.at[at], sem.at[i]))
        copies[-1].start()
    for copy in copies:
        copy.wait()


def on_device(teacher_batch, student_batch, positions, teacher_head, student_head):
    width_t, shard = teacher_head.shape
    width_s = student_head.shape[0]
    vocab = shard * NX * NZ
    wide = 128 * pl.cdiv(width_t + width_s, 128)
    groups = NY * NC
    hbm = pl.BlockSpec(memory_space=pltpu.HBM)
    in_hbm = functools.partial(pltpu.with_memory_space_constraint, memory_space=pltpu.HBM)
    vmem = pl.BlockSpec(memory_space=pltpu.VMEM)
    dma = pltpu.SemaphoreType.DMA
    grad, cols, loss = pl.pallas_call(
        functools.partial(exchange_kernel, vocab, width_t, width_s, shard),
        out_shape=(
            pltpu.VMEM((ROWS, shard), BF16),
            pltpu.VMEM((width_s, ROWS), BF16),
            pltpu.VMEM((1, 128), F32),
        ),
        in_specs=[hbm] * 5,
        out_specs=(vmem, vmem, vmem),
        scratch_shapes=[
            pltpu.VMEM(teacher_batch.shape, BF16),
            pltpu.VMEM(student_batch.shape, BF16),
            pltpu.VMEM((1, TOK), jnp.int32),
            pltpu.VMEM(teacher_head.shape, BF16),
            pltpu.VMEM(student_head.shape, BF16),
            pltpu.VMEM((NY, NC, TOK, wide), BF16),
            pltpu.VMEM((ROWS, wide), BF16),
            pltpu.VMEM((2, ROWS, shard), F32),
            pltpu.VMEM((2, NY, TOK, shard), F32),
            pltpu.VMEM((2, NY, TOK, shard), F32),
            pltpu.VMEM((2, TOK, shard), F32),
            pltpu.VMEM((2, TOK, shard), F32),
            pltpu.VMEM((2, 2, TOK, shard), F32),
            pltpu.VMEM((groups, 2, TOK, shard), F32),
            pltpu.VMEM((groups, 2, TOK, shard), F32),
            pltpu.VMEM((groups, 2, TOK, 128), F32),
            pltpu.VMEM((NZ, 128), F32),
            pltpu.VMEM((NX * groups, 128), F32),
            dma((5,)),
            dma((groups,)), dma((groups,)),
            dma((2, NY)), dma((2, NY)),
            dma((2,)), dma((2,)),
            dma((2, 2)), dma((2, 2)),
            dma((groups, 2)), dma((groups, 2)),
            dma((2,)), dma((2,)),
            pltpu.SemaphoreType.REGULAR,
            pltpu.SemaphoreType.REGULAR,
        ],
        compiler_params=pltpu.CompilerParams(
            collective_id=0, has_side_effects=True, vmem_limit_bytes=32 * 1024 * 1024
        ),
    )(*map(in_hbm, (teacher_batch, student_batch, positions.reshape(1, TOK), teacher_head, student_head)))
    pieces = 4
    head_grad, loss = pl.pallas_call(
        functools.partial(final_kernel, pieces),
        out_shape=(
            jax.ShapeDtypeStruct((width_s, shard), BF16),
            jax.ShapeDtypeStruct((1, TOK), F32),
        ),
        in_specs=[vmem] * 3,
        out_specs=(hbm, hbm),
        scratch_shapes=[pltpu.VMEM((width_s, shard), BF16), pltpu.VMEM((1, TOK), F32), dma((pieces + 1,))],
        compiler_params=pltpu.CompilerParams(vmem_limit_bytes=16 * 1024 * 1024),
    )(cols, grad, loss)
    return head_grad, loss.reshape(TOK)


def solution(mesh):
    in_specs = (P("tok", None), P("tok", None), P("tok"), P("tok", "voc"), P("tok", "voc"))
    out_specs = (P("tok", "voc"), P("tok"))
    return jax.shard_map(
        on_device, mesh=mesh, in_specs=in_specs, out_specs=out_specs, check_vma=False
    )
```
